32 devices in a mesh: dp: 4 (over z), expert: 4 (over x, core), mp: 2 (over y).
Axes of the slice: x: 2, y: 2, z: 4, core: 2. Of those that a mesh axis runs over, the one named last changes fastest.
Arguments:
- x_rows: bfloat16 [256, 3072], P(('dp', 'expert')), may hold values from -6 to 6, as said below
- dy_rows: bfloat16 [256, 3072], P(('dp', 'expert')), may hold values from -1.5 to 1.5, as said below
- w_in: bfloat16 [4, 3072, 2, 672], P('expert', None, None, 'mp'), may hold values from -0.109375 to 0.109375
- w_out: bfloat16 [4, 3072, 672], P('expert', None, 'mp'), may hold values from -0.25 to 0.25
- counts: int32 [16, 4], P(('dp', 'expert')), may hold values from 0 to 4, as said below
- assign: int32 [64, 2], P(('dp', 'expert')), may hold values from 0 to 3, as said below
Outputs:
- grad_w_in: bfloat16 [4, 3072, 2, 672], P('expert', 'dp', None, 'mp')
- grad_w_out: bfloat16 [4, 3072, 672], P('expert', 'dp', 'mp')
- grad_tokens: bfloat16 [64, 3072], P(('dp', 'expert'), 'mp')
The draws below stay inside these ranges and needn't reach their ends.
Inputs may be any that keep to these rules, and one draw needn't show every extreme that they name: counts[(g, u), s] is the number of tokens of owner s of group g that name expert e = u // 1 in assign, equal for the slices of one expert; it is at most 4, and 4 is reached in every group. `assign`: each token names 2 different experts; no owner names one expert for more than 4 of its tokens. `x_rows`: the 1 slices of one expert in one group keep equal copies of the same rows. `dy_rows`: the 1 slices of one expert in one group keep equal copies of the same rows.
All inputs are finite; a program needn't handle non-finite values.
Results may differ from the reference program's by a relative error of at most 0.018.
Values may be sent and summed in bfloat16 or wider, within the bound.
No kernel may reach another device: no remote copies, remote signals or barrier semaphores. Data moves between devices by JAX's collectives and lax.ppermute only.
A program may use at most 64 MiB of HBM per device.

```python
import jax
import jax.numpy as jnp
from jax import lax

D = 3072
TOK = 4
EXPERTS = 4
TOP = 2
SLICES = 1
OWNERS = 4
SLICE_FF = 672
FF_EXP = 672
HOT = 1
CAP = 4
ROWS = 16
N_DP = 4
N_EXPERT = 4


def expert_order(group_key):
    return jax.random.permutation(group_key, EXPERTS)


def token_columns(column_key):
    return jax.random.permutation(column_key, TOP)


def route_tables(base_key):
    owner_total = N_DP * OWNERS
    route_total = TOK * TOP
    cold_count = EXPERTS - HOT
    spare_rows = route_total - HOT * CAP
    group_keys = jax.random.split(jax.random.fold_in(base_key, 11), N_DP)
    owner_keys = jax.random.split(jax.random.fold_in(base_key, 12), owner_total)
    rank_order = jax.vmap(expert_order)(group_keys)

    def owner_counts(owner_key):
        chosen = (jax.random.permutation(owner_key, cold_count * CAP) < spare_rows).astype(jnp.int32)
        cold_rows = jnp.sum(chosen.reshape(cold_count, CAP), axis=1)
        return jnp.concatenate([jnp.full((HOT,), CAP, jnp.int32), cold_rows])
    by_rank = jax.vmap(owner_counts)(owner_keys).reshape(N_DP, OWNERS, EXPERTS)
    rank_of = jnp.argsort(rank_order, axis=1, stable=True).astype(jnp.int32)
    per_expert = jnp.take_along_axis(by_rank, jnp.broadcast_to(rank_of[:, None, :], by_rank.shape), axis=2)

    def owner_routes(count_row, owner_key):
        bounds = jnp.cumsum(count_row)
        ordered = jnp.searchsorted(bounds, jnp.arange(route_total, dtype=jnp.int32), side='right').astype(jnp.int32)
        routes = ordered.reshape(TOP, TOK).T
        token_order = jax.random.permutation(jax.random.fold_in(owner_key, 1), TOK)
        column_keys = jax.random.split(jax.random.fold_in(owner_key, 2), TOK)
        column_order = jax.vmap(token_columns)(column_keys)
        return jnp.take_along_axis(routes[token_order], column_order, axis=1)
    routes_all = jax.vmap(owner_routes)(per_expert.reshape(owner_total, EXPERTS), owner_keys)
    assign = routes_all.reshape(owner_total * TOK, TOP).astype(jnp.int32)
    by_expert = jnp.transpose(per_expert, (0, 2, 1))
    counts = jnp.repeat(by_expert, SLICES, axis=1).reshape(N_DP * N_EXPERT, OWNERS).astype(jnp.int32)
    return (assign, counts)


def slice_copies(key, scale, bound):
    base = jnp.clip(scale * jax.random.normal(key, (N_DP, EXPERTS, 1, ROWS, D), jnp.float32), -bound, bound)
    tiled = jnp.broadcast_to(base, (N_DP, EXPERTS, SLICES, ROWS, D))
    return tiled.reshape(N_DP * N_EXPERT * ROWS, D).astype(jnp.bfloat16)


def draw_x_rows(key, part):
    key = jax.random.fold_in(key, 21)
    return slice_copies(key, 1.0, 6.0)


def draw_dy_rows(key, part):
    key = jax.random.fold_in(key, 22)
    return slice_copies(key, 0.25, 1.5)


def draw_counts(key, part):
    return route_tables(key)[1]


def draw_assign(key, part):
    return route_tables(key)[0]


def level_of(own_key, dims, cuts, smallest, top_value):
    def one(axis_at, parts):
        heights = jax.random.uniform(jax.random.fold_in(jax.random.fold_in(own_key, 6), axis_at), (parts,), jnp.float32, smallest / len(cuts), top_value / len(cuts))
        return jnp.repeat(jnp.exp(heights), dims[axis_at] // parts).reshape((-1,) + (1,) * (len(dims) - axis_at - 1))

    level = one(*cuts[0])
    for cut in cuts[1:]:
        level = level * one(*cut)
    return level


def bell_draw(key, shape, scale, reach, cuts=(), kind=jnp.bfloat16):
    values = scale * jax.random.normal(key, shape, jnp.float32)
    if cuts:
        values = values * level_of(key, shape, cuts, -0.22, 0.18)
    return jnp.clip(values, -reach, reach).astype(kind)


def setup_inputs(seed: int = 0) -> dict:
    streams_of = jax.random.split(jax.random.key(seed), 7)
    return {
        "x_rows": draw_x_rows(jax.random.fold_in(streams_of[6], 71), 0),
        "dy_rows": draw_dy_rows(jax.random.fold_in(streams_of[6], 71), 0),
        "w_in": bell_draw(streams_of[2], (N_EXPERT, D, 2, SLICE_FF), D ** -0.5, 0.109375, ((0, 4), (3, 2))),
        "w_out": bell_draw(streams_of[3], (N_EXPERT, D, SLICE_FF), FF_EXP ** -0.5, 0.25, ((0, 4), (2, 2))),
        "counts": draw_counts(jax.random.fold_in(streams_of[6], 71), 0),
        "assign": draw_assign(jax.random.fold_in(streams_of[6], 71), 0),
    }


def expert_rows(x_block, dy_block, w_flat, w_down, live_mask):
    preact = jnp.dot(x_block, w_flat, preferred_element_type=jnp.float32)
    gate_pre = preact[:, :SLICE_FF]
    up_pre = preact[:, SLICE_FF:]
    sigmoid_gate = jax.nn.sigmoid(gate_pre)
    hidden = (live_mask * gate_pre * sigmoid_gate * up_pre).astype(jnp.bfloat16)
    grad_hidden = jnp.dot(dy_block, w_down, preferred_element_type=jnp.float32)
    grad_gate = live_mask * grad_hidden * up_pre * sigmoid_gate * (1.0 + gate_pre * (1.0 - sigmoid_gate))
    grad_up = live_mask * grad_hidden * gate_pre * sigmoid_gate
    grad_pre = jnp.concatenate([grad_gate, grad_up], axis=1).astype(jnp.bfloat16)
    row_parts = lax.dot_general(grad_pre, w_flat, (((1,), (1,)), ((), ())), preferred_element_type=jnp.float32).astype(jnp.bfloat16)
    term_in = lax.dot_general(x_block, grad_pre, (((0,), (0,)), ((), ())), preferred_element_type=jnp.float32).astype(jnp.bfloat16)
    term_out = lax.dot_general(dy_block, hidden, (((0,), (0,)), ((), ())), preferred_element_type=jnp.float32).astype(jnp.bfloat16)
    return row_parts, term_in, term_out


def reference(x_rows, dy_rows, w_in, w_out, counts, assign):
    live_total = jnp.sum(counts, axis=1).reshape(N_DP, N_EXPERT)
    x_groups = x_rows.reshape(N_DP, N_EXPERT, ROWS, D)
    dy_groups = dy_rows.reshape(N_DP, N_EXPERT, ROWS, D)
    slot_index = jnp.arange(ROWS, dtype=jnp.int32)

    def per_slice(slice_index):
        w_flat = w_in[slice_index].reshape(D, 2 * SLICE_FF)
        w_down = w_out[slice_index]
        row_list = []
        total_in = jnp.zeros((D, 2 * SLICE_FF), jnp.float32)
        total_out = jnp.zeros((D, SLICE_FF), jnp.float32)
        for replica in range(N_DP):
            live_mask = (slot_index < live_total[replica, slice_index]).astype(jnp.float32)[:, None]
            row_parts, term_in, term_out = expert_rows(x_groups[replica, slice_index], dy_groups[replica, slice_index], w_flat, w_down, live_mask)
            row_list.append(row_parts)
            total_in = total_in + lax.optimization_barrier(term_in).astype(jnp.float32)
            total_out = total_out + lax.optimization_barrier(term_out).astype(jnp.float32)
        grad_in = total_in.astype(jnp.bfloat16).reshape(D, 2, SLICE_FF)
        return jnp.stack(row_list), grad_in, total_out.astype(jnp.bfloat16)

    all_rows, grad_w_in, grad_w_out = lax.map(per_slice, jnp.arange(N_EXPERT, dtype=jnp.int32))
    count_cube = counts.reshape(N_DP, N_EXPERT, OWNERS)[:, ::SLICES]
    offsets = (jnp.cumsum(count_cube, axis=2) - count_cube).astype(jnp.int32)
    flat_routes = assign.reshape(N_DP, OWNERS, TOK * TOP).astype(jnp.int32)
    same_expert = flat_routes[:, :, :, None] == flat_routes[:, :, None, :]
    token_of = jnp.arange(TOK * TOP, dtype=jnp.int32) // TOP
    earlier = token_of[None, :] < token_of[:, None]
    route_rank = jnp.sum((same_expert & earlier[None, None]).astype(jnp.int32), axis=3)
    replica_index = jnp.arange(N_DP, dtype=jnp.int32)[:, None, None]
    owner_index = jnp.arange(OWNERS, dtype=jnp.int32)[None, :, None]
    slot_start = offsets[replica_index, flat_routes, owner_index]
    slice_ids = jnp.arange(SLICES, dtype=jnp.int32)[None, None, None, :]
    unit = flat_routes[..., None] * SLICES + slice_ids
    row_index = ((unit * N_DP + replica_index[..., None]) * ROWS + (slot_start + route_rank)[..., None]).astype(jnp.int32)
    picked = all_rows.reshape(N_EXPERT * N_DP * ROWS, D)[row_index]
    summed = jnp.sum(picked.astype(jnp.float32).reshape(N_DP, OWNERS, TOK, TOP * SLICES, D), axis=3)
    grad_tokens = summed.astype(jnp.bfloat16).reshape(N_DP * OWNERS * TOK, D)
    return grad_w_in, grad_w_out, grad_tokens
```

```python
import jax
import jax.numpy as jnp
from jax import lax
from jax.sharding import PartitionSpec as P

LAYER_EXPERTS = 16
BF16 = jnp.bfloat16
F32 = jnp.float32


def local_grads(x_rows, dy_rows, w_flat, w_down, live_mask, pick):
    hidden_units = w_down.shape[0]
    contract_last = (((1,), (1,)), ((), ()))
    preact = lax.dot_general(x_rows, w_flat, contract_last, preferred_element_type=F32)
    gate_pre = preact[:, :hidden_units]
    up_pre = preact[:, hidden_units:]
    sigmoid_gate = jax.nn.sigmoid(gate_pre)
    hidden = (live_mask * gate_pre * sigmoid_gate * up_pre).astype(BF16)
    grad_hidden = lax.dot_general(dy_rows, w_down, contract_last, preferred_element_type=F32)
    grad_gate = (
        live_mask * grad_hidden * up_pre * sigmoid_gate * (1.0 + gate_pre * (1.0 - sigmoid_gate))
    )
    grad_up = live_mask * grad_hidden * gate_pre * sigmoid_gate
    grad_pre = jnp.concatenate([grad_gate, grad_up], axis=1).astype(BF16)
    picked = jnp.dot(pick, grad_pre, preferred_element_type=F32).astype(BF16)
    row_parts = jnp.dot(picked, w_flat, preferred_element_type=F32).astype(BF16)
    return jnp.concatenate([grad_pre, hidden], axis=1), row_parts


def pick_matrix(per_source, slot_total):
    owners = per_source.shape[0]
    capacity = slot_total // owners
    offsets = jnp.cumsum(per_source) - per_source
    lane = jnp.arange(capacity, dtype=jnp.int32)
    wanted = jnp.where(lane[None, :] < per_source[:, None], offsets[:, None] + lane[None, :], -1)
    slots = jnp.arange(slot_total, dtype=jnp.int32)
    return (wanted.reshape(-1)[:, None] == slots[None, :]).astype(BF16)


def token_selector(assign, units, parts, capacity):
    slices = units // min(LAYER_EXPERTS, units)
    tokens, route_width = assign.shape
    flat_routes = assign.reshape(-1)
    token_of = jnp.arange(flat_routes.shape[0], dtype=jnp.int32) // route_width
    same_expert = flat_routes[:, None] == flat_routes[None, :]
    earlier = token_of[None, :] < token_of[:, None]
    route_rank = jnp.sum((same_expert & earlier).astype(jnp.int32), axis=1)
    columns = jnp.arange(units * parts * capacity, dtype=jnp.int32)
    column_expert = columns // (capacity * parts * slices)
    column_rank = columns % capacity
    hits = (column_expert[None, :] == flat_routes[:, None]) & (
        column_rank[None, :] == route_rank[:, None]
    )
    return jnp.sum(hits.astype(F32).reshape(tokens, route_width, -1), axis=1).astype(BF16)


def per_device(x_rows, dy_rows, w_in, w_out, counts, assign):
    slot_total, model_width = x_rows.shape
    hidden_units = w_out.shape[2]
    groups = lax.axis_size("dp")
    units = lax.axis_size("expert")
    parts = lax.axis_size("mp")
    owners = counts.shape[1]
    capacity = slot_total // owners
    quarter = model_width // groups
    share = model_width // parts

    both = jnp.concatenate([x_rows, dy_rows], axis=0)
    both_all = lax.all_to_all(both, "dp", split_axis=1, concat_axis=0, tiled=True)
    both_all = both_all.reshape(groups, 2, slot_total, quarter)

    w_flat = jnp.transpose(w_in[0], (1, 2, 0)).reshape(2 * hidden_units, model_width)
    w_down = jnp.transpose(w_out[0], (1, 0))
    per_source = counts[0]
    slot_index = jnp.arange(slot_total, dtype=jnp.int32)
    live_mask = (slot_index < jnp.sum(per_source)).astype(F32)[:, None]
    pick = pick_matrix(per_source, slot_total)
    acts, row_parts = local_grads(x_rows, dy_rows, w_flat, w_down, live_mask, pick)

    acts_all = lax.all_to_all(
        jnp.broadcast_to(acts[None], (groups,) + acts.shape), "dp", 0, 0, tiled=True
    ).reshape(groups * slot_total, 3 * hidden_units)

    outgoing = row_parts.reshape(units, capacity, parts, share).transpose(0, 2, 1, 3)
    incoming = lax.all_to_all(
        outgoing.reshape(units * parts, capacity, share), ("expert", "mp"), 0, 0, tiled=True
    )
    selector = token_selector(assign, units, parts, capacity)
    grad_tokens = jnp.dot(
        selector, incoming.reshape(units * parts * capacity, share), preferred_element_type=F32
    ).astype(BF16)

    contract_first = (((0,), (0,)), ((), ()))
    x_all = both_all[:, 0].reshape(groups * slot_total, quarter)
    dy_all = both_all[:, 1].reshape(groups * slot_total, quarter)
    grad_in = lax.dot_general(
        acts_all[:, : 2 * hidden_units], x_all, contract_first, preferred_element_type=F32
    ).astype(BF16)
    grad_out = lax.dot_general(
        acts_all[:, 2 * hidden_units :], dy_all, contract_first, preferred_element_type=F32
    ).astype(BF16)
    grad_w_in = grad_in.reshape(2, hidden_units, quarter).transpose(2, 0, 1)[None]
    grad_w_out = grad_out.transpose(1, 0)[None]
    return (grad_w_in, grad_w_out, grad_tokens)


def solution(mesh):
    return jax.shard_map(
        per_device,
        mesh=mesh,
        in_specs=(
            P(("dp", "expert"), None),
            P(("dp", "expert"), None),
            P("expert", None, None, "mp"),
            P("expert", None, "mp"),
            P(("dp", "expert"), None),
            P(("dp", "expert"), None),
        ),
        out_specs=(
            P("expert", "dp", None, "mp"),
            P("expert", "dp", "mp"),
            P(("dp", "expert"), "mp"),
        ),
        check_vma=False,
    )
```

```python
import functools

import jax
import jax.numpy as jnp
from jax import lax
from jax.experimental import pallas as pl
from jax.experimental.pallas import tpu as pltpu
from jax.sharding import PartitionSpec as P

LAYER_EXPERTS = 16
DIRECT_PEERS = 16
BF16 = jnp.bfloat16
F32 = jnp.float32
VMEM_BYTES = 48 * 1024 * 1024
CONTRACT_LAST = (((1,), (1,)), ((), ()))

ANY = pl.BlockSpec(memory_space=pl.ANY)
IN_VMEM = pl.BlockSpec(memory_space=pltpu.VMEM)
IN_SMEM = pl.BlockSpec(memory_space=pltpu.SMEM)


def cuts_of(rows, most=256, unit=16):
    pieces = -(-rows // most)
    size = -(-rows // pieces)
    size = -(-size // unit) * unit
    return [(at, min(size, rows - at)) for at in range(0, rows, size)]


def split_kernel(groups, x_ref, dy_ref, *rest):
    outs, sems = rest[:groups], rest[groups]
    rows, width = x_ref.shape
    quarter = width // groups
    me = lax.axis_index("dp")
    copies = []
    for step in range(groups):
        goal = lax.rem(me + step, groups)
        columns = pl.ds(pl.multiple_of(goal * quarter, quarter), quarter)
        for half, ref in enumerate((x_ref, dy_ref)):
            copy = pltpu.make_async_copy(
                ref.at[:, columns],
                outs[step].at[pl.ds(half * rows, rows), :],
                sems.at[2 * step + half],
            )
            copy.start()
            copies.append(copy)
    for copy in copies:
        copy.wait()


def acts_kernel(units, parts, direct, *refs):
    x_hbm, dy_hbm, w_in_hbm, w_out_hbm, counts_hbm = refs[:5]
    blocks = units * parts if direct else 1
    acts_ref, row_refs = refs[5], refs[6 : 6 + blocks]
    x_ref, dy_ref, w_in_ref, w_out_ref, counts_ref, rows_ref, sems = refs[6 + blocks :]

    in_cuts = cuts_of(w_in_ref.shape[0])
    out_cuts = cuts_of(w_out_ref.shape[0])
    plan = [(counts_hbm, counts_ref), (x_hbm, x_ref)]
    plan += [(w_in_hbm.at[pl.ds(a, n), :], w_in_ref.at[pl.ds(a, n), :]) for a, n in in_cuts]
    plan += [(dy_hbm, dy_ref)]
    plan += [(w_out_hbm.at[pl.ds(a, n), :], w_out_ref.at[pl.ds(a, n), :]) for a, n in out_cuts]
    copies = [pltpu.make_async_copy(s, d, sems.at[i]) for i, (s, d) in enumerate(plan)]
    for copy in copies:
        copy.start()
    copies = iter(copies)

    next(copies).wait()
    slots = x_ref.shape[0]
    owners = counts_ref.shape[1]
    capacity = slots // owners
    my_unit = lax.axis_index("expert") if direct else 0
    row_at = lax.broadcasted_iota(jnp.int32, (slots, slots), 0)
    slot_at = lax.broadcasted_iota(jnp.int32, (slots, slots), 1)
    pick = jnp.zeros((slots, slots), F32)
    total = jnp.int32(0)
    for owner in range(owners):
        held = counts_ref[0, owner]
        first = lax.rem(owner - my_unit + owners, owners) * capacity
        hit = (row_at >= first) & (row_at < first + held) & (slot_at - row_at == total - first)
        pick = jnp.where(hit, 1.0, pick)
        total = total + held

    next(copies).wait()
    x = x_ref[...]
    pre = []
    for at, size in in_cuts:
        next(copies).wait()
        pre.append(
            lax.dot_general(
                x, w_in_ref[pl.ds(at, size), :], CONTRACT_LAST, preferred_element_type=F32
            )
        )
    pre = jnp.concatenate(pre, axis=1)
    next(copies).wait()
    dy = dy_ref[...]
    grad_hidden = []
    for at, size in out_cuts:
        next(copies).wait()
        grad_hidden.append(
            lax.dot_general(
                dy, w_out_ref[pl.ds(at, size), :], CONTRACT_LAST, preferred_element_type=F32
            )
        )
    grad_hidden = jnp.concatenate(grad_hidden, axis=1)

    units_here = w_out_ref.shape[0]
    gate_pre, up_pre = pre[:, :units_here], pre[:, units_here:]
    live = lax.broadcasted_iota(jnp.int32, gate_pre.shape, 0) < total
    live_mask = jnp.where(live, 1.0, 0.0)
    sigmoid_gate = jax.nn.sigmoid(gate_pre)
    hidden = live_mask * gate_pre * sigmoid_gate * up_pre
    grad_gate = (
        live_mask * grad_hidden * up_pre * sigmoid_gate * (1.0 + gate_pre * (1.0 - sigmoid_gate))
    )
    grad_up = live_mask * grad_hidden * gate_pre * sigmoid_gate
    grad_pre = jnp.concatenate([grad_gate, grad_up], axis=1).astype(BF16)
    acts_ref[...] = jnp.concatenate([grad_gate, grad_up, hidden], axis=1).astype(BF16)

    picked = jnp.dot(pick.astype(BF16), grad_pre, preferred_element_type=F32).astype(BF16)
    width = w_in_ref.shape[1]
    for at, size in cuts_of(width, 512, 128):
        rows_ref[:, pl.ds(at, size)] = jnp.dot(
            picked, w_in_ref[:, pl.ds(at, size)], preferred_element_type=F32
        )
    share = width // parts
    my_part = lax.axis_index("mp") if direct else 0
    for other in range(parts):
        goal = lax.rem(my_part + other, parts)
        half = rows_ref[:, pl.ds(pl.multiple_of(goal * share, share), share)].astype(BF16)
        for unit in range(units):
            piece = half[unit * capacity : (unit + 1) * capacity]
            index = unit * parts + other
            if direct:
                row_refs[index][...] = piece
            else:
                row_refs[0][index] = piece


def weights_kernel(groups, *refs):
    sent, acts = refs[:groups], refs[groups : 2 * groups]
    in_hbm, out_hbm, in_ref, out_ref, sems = refs[2 * groups :]
    slots = acts[0].shape[0]
    x = jnp.concatenate([ref[:slots] for ref in sent], axis=0)
    dy = jnp.concatenate([ref[slots:] for ref in sent], axis=0)
    columns = jnp.concatenate([ref[...] for ref in acts], axis=0).T
    copies = []
    start = 0
    for values, target, staged in ((x, in_hbm, in_ref), (dy, out_hbm, out_ref)):
        for at, size in cuts_of(target.shape[0]):
            here = pl.ds(at, size)
            staged[here, :] = jnp.dot(
                columns[start + at : start + at + size], values, preferred_element_type=F32
            ).astype(BF16)
            copy = pltpu.make_async_copy(
                staged.at[here, :], target.at[here, :], sems.at[len(copies)]
            )
            copy.start()
            copies.append(copy)
        start += target.shape[0]
    for copy in copies:
        copy.wait()


def tokens_kernel(units, parts, direct, capacity, assign_ref, *refs):
    out_ref, rows_ref = refs[-2:]
    pieces = refs[:-2]
    count = units * parts
    for index in range(count):
        piece = pieces[index][...] if direct else pieces[0][index]
        rows_ref[pl.ds(index * capacity, capacity), :] = piece.astype(F32)
    width, tokens = assign_ref.shape
    slices = units // min(LAYER_EXPERTS, units)
    token_at = lax.broadcasted_iota(jnp.int32, (tokens, count * capacity), 0)
    column_at = lax.broadcasted_iota(jnp.int32, (tokens, count * capacity), 1)
    selector = jnp.zeros((tokens, count * capacity), F32)
    my_unit = lax.axis_index("expert") if direct else 0
    for token in range(tokens):
        for k in range(width):
            expert = assign_ref[k, token]
            rank = jnp.int32(0)
            for earlier in range(token):
                for other in range(width):
                    rank = rank + (assign_ref[other, earlier] == expert).astype(jnp.int32)
            for piece in range(slices):
                source = expert * slices + piece
                if direct:
                    source = lax.rem(my_unit - source + units, units)
                for part in range(parts):
                    column = (source * parts + part) * capacity + rank
                    hit = (token_at == token) & (column_at == column)
                    selector = jnp.where(hit, selector + 1.0, selector)
    out_ref[...] = jnp.dot(
        selector.astype(BF16), rows_ref[...].astype(BF16), preferred_element_type=F32
    ).astype(BF16)


def params():
    return pltpu.CompilerParams(vmem_limit_bytes=VMEM_BYTES)


def shift_along(array, axis, step):
    size = lax.axis_size(axis)
    return lax.ppermute(array, axis, [(i, (i + step) % size) for i in range(size)])


def per_device(x_rows, dy_rows, w_in, w_out, counts, assign):
    slots, width = x_rows.shape
    hidden_units = w_out.shape[2]
    groups = lax.axis_size("dp")
    units = lax.axis_size("expert")
    parts = lax.axis_size("mp")
    capacity = slots // counts.shape[1]
    quarter = width // groups
    share = width // parts
    peers = units * parts
    direct = peers <= DIRECT_PEERS
    shape = jax.ShapeDtypeStruct

    split = pl.pallas_call(
        functools.partial(split_kernel, groups),
        out_shape=[shape((2 * slots, quarter), BF16)] * groups,
        in_specs=[ANY, ANY],
        out_specs=[ANY] * groups,
        scratch_shapes=[pltpu.SemaphoreType.DMA((2 * groups,))],
        compiler_params=params(),
        name="split_rows",
    )(x_rows, dy_rows)
    sent = [split[0]] + [shift_along(split[s], "dp", s) for s in range(1, groups)]

    w_flat = jnp.transpose(w_in[0], (1, 2, 0)).reshape(2 * hidden_units, width)
    w_down = jnp.transpose(w_out[0], (1, 0))
    if direct:
        row_shapes = [shape((capacity, share), BF16)] * peers
    else:
        row_shapes = [shape((peers, capacity, share), BF16)]
    copies = 3 + len(cuts_of(2 * hidden_units)) + len(cuts_of(hidden_units))
    acts, *row_parts = pl.pallas_call(
        functools.partial(acts_kernel, units, parts, direct),
        out_shape=[shape((slots, 3 * hidden_units), BF16)] + row_shapes,
        in_specs=[ANY] * 5,
        out_specs=[IN_VMEM] * (1 + len(row_shapes)),
        scratch_shapes=[
            pltpu.VMEM(x_rows.shape, BF16),
            pltpu.VMEM(dy_rows.shape, BF16),
            pltpu.VMEM(w_flat.shape, BF16),
            pltpu.VMEM(w_down.shape, BF16),
            pltpu.SMEM(counts.shape, jnp.int32),
            pltpu.VMEM((slots, width), F32),
            pltpu.SemaphoreType.DMA((copies,)),
        ],
        compiler_params=params(),
        name="acts_and_rows",
    )(x_rows, dy_rows, w_flat, w_down, counts)

    acts_all = [acts] + [shift_along(acts, "dp", s) for s in range(1, groups)]
    if direct:
        incoming = []
        for unit in range(units):
            for part in range(parts):
                piece = row_parts[unit * parts + part]
                if unit or part:
                    pairs = [
                        (e * parts + m, (e + unit) % units * parts + (m + part) % parts)
                        for e in range(units)
                        for m in range(parts)
                    ]
                    piece = lax.ppermute(piece, ("expert", "mp"), pairs)
                incoming.append(piece)
    else:
        incoming = [lax.all_to_all(row_parts[0], ("expert", "mp"), 0, 0, tiled=True)]

    grad_in, grad_out = pl.pallas_call(
        functools.partial(weights_kernel, groups),
        out_shape=[
            shape((2 * hidden_units, quarter), BF16),
            shape((hidden_units, quarter), BF16),
        ],
        in_specs=[IN_VMEM] * (2 * groups),
        out_specs=[ANY, ANY],
        scratch_shapes=[
            pltpu.VMEM((2 * hidden_units, quarter), BF16),
            pltpu.VMEM((hidden_units, quarter), BF16),
            pltpu.SemaphoreType.DMA((len(cuts_of(2 * hidden_units)) + len(cuts_of(hidden_units)),)),
        ],
        compiler_params=params(),
        name="weight_grads",
    )(*sent, *acts_all)

    grad_tokens = pl.pallas_call(
        functools.partial(tokens_kernel, units, parts, direct, capacity),
        out_shape=shape((assign.shape[0], share), BF16),
        in_specs=[IN_SMEM] + [IN_VMEM] * len(incoming),
        out_specs=IN_VMEM,
        scratch_shapes=[pltpu.VMEM((peers * capacity, share), F32)],
        compiler_params=params(),
        name="token_grads",
    )(assign.T, *incoming)

    grad_w_in = grad_in.reshape(2, hidden_units, quarter).transpose(2, 0, 1)[None]
    grad_w_out = grad_out.transpose(1, 0)[None]
    return (grad_w_in, grad_w_out, grad_tokens)


def solution(mesh):
    return jax.shard_map(
        per_device,
        mesh=mesh,
        in_specs=(
            P(("dp", "expert"), None),
            P(("dp", "expert"), None),
            P("expert", None, None, "mp"),
            P("expert", None, "mp"),
            P(("dp", "expert"), None),
            P(("dp", "expert"), None),
        ),
        out_specs=(
            P("expert", "dp", None, "mp"),
            P("expert", "dp", "mp"),
            P(("dp", "expert"), "mp"),
        ),
        check_vma=False,
    )
```

```python
import functools

import jax
import jax.numpy as jnp
from jax import lax
from jax.experimental import pallas as pl
from jax.experimental.pallas import tpu as pltpu
from jax.sharding import PartitionSpec as P

LAYER_EXPERTS = 16
BF16 = jnp.bfloat16
F32 = jnp.float32
VMEM_BYTES = 48 * 1024 * 1024
CONTRACT_LAST = (((1,), (1,)), ((), ()))

ANY = pl.BlockSpec(memory_space=pl.ANY)
IN_HBM = pl.BlockSpec(memory_space=pltpu.HBM)
IN_VMEM = pl.BlockSpec(memory_space=pltpu.VMEM)
IN_SMEM = pl.BlockSpec(memory_space=pltpu.SMEM)


def shape(dims, dtype=BF16):
    return jax.ShapeDtypeStruct(dims, dtype)


def params():
    return pltpu.CompilerParams(vmem_limit_bytes=VMEM_BYTES)


def bits_of(size):
    return size.bit_length() - 1


def cuts_of(rows, most=256, unit=16):
    pieces = -(-rows // most)
    size = -(-rows // pieces)
    size = -(-size // unit) * unit
    return [(at, min(size, rows - at)) for at in range(0, rows, size)]


def column_start(me, bits, step, width, flipped):
    place = lax.shift_right_logical(me, jnp.int32(bits - 1 - step))
    if flipped:
        place = place ^ 1
    return place * (width // 2 ** (step + 1))


def lanes(start, size):
    return pl.ds(pl.multiple_of(start, 128), size)


def split_kernel(bits, x_ref, dy_ref, *rest):
    outs, sems = rest[: bits + 1], rest[bits + 1]
    rows, width = x_ref.shape
    me = lax.axis_index("dp")
    copies = []
    for step in range(bits + 1):
        own = step == bits
        last = min(step, bits - 1)
        start = column_start(me, bits, last, width, not own)
        size = width // 2 ** (last + 1)
        for half, ref in enumerate((x_ref, dy_ref)):
            copy = pltpu.make_async_copy(
                ref.at[:, lanes(start, size)],
                outs[step].at[pl.ds(half * rows, rows), :],
                sems.at[2 * step + half],
            )
            copy.start()
            copies.append(copy)
    for copy in copies:
        copy.wait()


def acts_kernel(parts, *refs):
    x_hbm, dy_hbm, w_in_hbm, w_out_hbm, counts_hbm = refs[:5]
    acts_ref, keep_ref, send_ref = refs[5:8]
    x_ref, dy_ref, w_in_ref, w_out_ref, counts_ref, rows_ref, sems = refs[8:]

    in_cuts = cuts_of(w_in_ref.shape[0])
    out_cuts = cuts_of(w_out_ref.shape[0])
    plan = [(x_hbm, x_ref)]
    plan += [(w_in_hbm.at[pl.ds(a, n), :], w_in_ref.at[pl.ds(a, n), :]) for a, n in in_cuts]
    plan += [(dy_hbm, dy_ref)]
    plan += [(w_out_hbm.at[pl.ds(a, n), :], w_out_ref.at[pl.ds(a, n), :]) for a, n in out_cuts]
    plan += [(counts_hbm, counts_ref)]
    copies = [pltpu.make_async_copy(s, d, sems.at[i]) for i, (s, d) in enumerate(plan)]
    for copy in copies:
        copy.start()
    copies = iter(copies)

    next(copies).wait()
    x = x_ref[...]
    pre = []
    for at, size in in_cuts:
        next(copies).wait()
        pre.append(
            lax.dot_general(
                x, w_in_ref[pl.ds(at, size), :], CONTRACT_LAST, preferred_element_type=F32
            )
        )
    pre = jnp.concatenate(pre, axis=1)
    next(copies).wait()
    dy = dy_ref[...]
    grad_hidden = []
    for at, size in out_cuts:
        next(copies).wait()
        grad_hidden.append(
            lax.dot_general(
                dy, w_out_ref[pl.ds(at, size), :], CONTRACT_LAST, preferred_element_type=F32
            )
        )
    grad_hidden = jnp.concatenate(grad_hidden, axis=1)

    next(copies).wait()
    slots = x_ref.shape[0]
    owners = counts_ref.shape[1]
    capacity = slots // owners
    my_unit = lax.axis_index("expert")
    row_at = lax.broadcasted_iota(jnp.int32, (slots, slots), 0)
    slot_at = lax.broadcasted_iota(jnp.int32, (slots, slots), 1)
    pick = jnp.zeros((slots, slots), F32)
    total = jnp.int32(0)
    for owner in range(owners):
        held = counts_ref[0, owner]
        first = (my_unit ^ owner) * capacity
        hit = (row_at >= first) & (row_at < first + held) & (slot_at - row_at == total - first)
        pick = jnp.where(hit, 1.0, pick)
        total = total + held

    units_here = w_out_ref.shape[0]
    gate_pre, up_pre = pre[:, :units_here], pre[:, units_here:]
    live = lax.broadcasted_iota(jnp.int32, gate_pre.shape, 0) < total
    live_mask = jnp.where(live, 1.0, 0.0)
    sigmoid_gate = jax.nn.sigmoid(gate_pre)
    hidden = live_mask * gate_pre * sigmoid_gate * up_pre
    grad_gate = (
        live_mask * grad_hidden * up_pre * sigmoid_gate * (1.0 + gate_pre * (1.0 - sigmoid_gate))
    )
    grad_up = live_mask * grad_hidden * gate_pre * sigmoid_gate
    grad_pre = jnp.concatenate([grad_gate, grad_up], axis=1).astype(BF16)
    acts_ref[...] = jnp.concatenate([grad_gate, grad_up, hidden], axis=1).astype(BF16)

    picked = jnp.dot(pick.astype(BF16), grad_pre, preferred_element_type=F32).astype(BF16)
    width = w_in_ref.shape[1]
    for at, size in cuts_of(width, 512, 128):
        rows_ref[:, pl.ds(at, size)] = jnp.dot(
            picked, w_in_ref[:, pl.ds(at, size)], preferred_element_type=F32
        )
    my_part = lax.axis_index("mp")
    bits = bits_of(parts)
    keep_ref[...] = rows_ref[:, lanes(column_start(my_part, bits, 0, width, False), width // 2)]
    send_ref[...] = rows_ref[
        :, lanes(column_start(my_part, bits, 0, width, True), width // 2)
    ].astype(BF16)


def sum_task(bits, step, width):
    def body(ins, outs):
        keep_ref, recv_ref = ins
        total = keep_ref[...].astype(F32) + recv_ref[...].astype(F32)
        if step + 1 < bits:
            me = lax.axis_index("mp")
            base = column_start(me, bits, step, width, False)
            size = width // 2 ** (step + 2)
            is_high = column_start(me, bits, step + 1, width, False) - base > 0
            low, high = total[:, :size], total[:, size:]
            outs[0][...] = jnp.where(is_high, high, low)
            outs[1][...] = jnp.where(is_high, low, high).astype(BF16)
        else:
            half = total.shape[0] // 2
            outs[0][...] = total[:half]
            outs[1][...] = total[half:].astype(BF16)

    return body


def deal_task(blocks, block):
    def body(ins, outs):
        keep, recv = ins[0][...].astype(F32), ins[1][...].astype(F32)
        joined = []
        for at in range(blocks):
            joined += [keep[at * block : (at + 1) * block], recv[at * block : (at + 1) * block]]
        outs[0][...] = jnp.concatenate(joined[:blocks], axis=0)
        outs[1][...] = jnp.concatenate(joined[blocks:], axis=0).astype(BF16)

    return body


def stack_task(ins, outs):
    at = 0
    for ref in ins:
        outs[0][pl.ds(at, ref.shape[0]), :] = ref[...]
        at += ref.shape[0]


def columns_task(bits, step, width):
    def body(ins, outs):
        me = lax.axis_index("dp")
        size = width // 2 ** (step + 1)
        start = column_start(me, bits, step, width, True)
        rows = ins[0].shape[0]
        outs[0][pl.ds(0, rows), :] = ins[0][...]
        at = rows
        for past, ref in enumerate(ins[1:]):
            base = column_start(me, bits, past, width, False)
            outs[0][pl.ds(at, ref.shape[0]), :] = ref[:, lanes(start - base, size)]
            at += ref.shape[0]

    return body


def run_tasks(tasks, name):
    ins = [array for _, arrays, _ in tasks for array in arrays]
    outs = [out for _, _, out_shapes in tasks for out in out_shapes]

    def kernel(*refs):
        in_at, out_at = 0, len(ins)
        for body, arrays, out_shapes in tasks:
            body(
                refs[in_at : in_at + len(arrays)],
                refs[out_at : out_at + len(out_shapes)],
            )
            in_at += len(arrays)
            out_at += len(out_shapes)

    results = iter(
        pl.pallas_call(
            kernel,
            out_shape=outs,
            in_specs=[IN_VMEM] * len(ins),
            out_specs=[IN_VMEM] * len(outs),
            compiler_params=params(),
            name=name,
        )(*ins)
    )
    return [[next(results) for _ in out_shapes] for _, _, out_shapes in tasks]


def weights_kernel(bits, width, *refs):
    count = 1 + bits
    sent, acts = refs[:count], refs[count : 2 * count]
    in_hbm, out_hbm, in_ref, out_ref, sems = refs[2 * count :]
    slots = acts[0].shape[0]
    me = lax.axis_index("dp")
    quarter = width // 2**bits
    x, dy = [], []
    for index, ref in enumerate(sent):
        if index == 0:
            block = ref[...]
        else:
            base = column_start(me, bits, index - 1, width, False)
            block = ref[:, lanes(me * quarter - base, quarter)]
        for at in range(0, block.shape[0], 2 * slots):
            x.append(block[at : at + slots])
            dy.append(block[at + slots : at + 2 * slots])
    x, dy = jnp.concatenate(x, axis=0), jnp.concatenate(dy, axis=0)
    columns = jnp.concatenate([ref[...] for ref in acts], axis=0).T
    copies = []
    start = 0
    for values, target, staged in ((x, in_hbm, in_ref), (dy, out_hbm, out_ref)):
        for at, size in cuts_of(target.shape[0]):
            here = pl.ds(at, size)
            staged[here, :] = jnp.dot(
                columns[start + at : start + at + size], values, preferred_element_type=F32
            ).astype(BF16)
            copy = pltpu.make_async_copy(
                staged.at[here, :], target.at[here, :], sems.at[len(copies)]
            )
            copy.start()
            copies.append(copy)
        start += target.shape[0]
    for copy in copies:
        copy.wait()


def tokens_kernel(units, capacity, assign_ref, keep_ref, recv_ref, out_ref):
    columns = units * capacity
    bits = bits_of(units)
    width, tokens = assign_ref.shape
    slices = units // min(LAYER_EXPERTS, units)
    token_at = lax.broadcasted_iota(jnp.int32, (tokens, columns), 0)
    column_at = lax.broadcasted_iota(jnp.int32, (tokens, columns), 1)
    selector = jnp.zeros((tokens, columns), F32)
    my_unit = lax.axis_index("expert")
    for token in range(tokens):
        for k in range(width):
            expert = assign_ref[k, token]
            rank = jnp.int32(0)
            for earlier in range(token):
                for other in range(width):
                    rank = rank + (assign_ref[other, earlier] == expert).astype(jnp.int32)
            for piece in range(slices):
                apart = (expert * slices + piece) ^ my_unit
                place = jnp.int32(0)
                for bit in range(bits):
                    place = place * 2 + (lax.shift_right_logical(apart, jnp.int32(bit)) & 1)
                hit = (token_at == token) & (column_at == place * capacity + rank)
                selector = jnp.where(hit, selector + 1.0, selector)
    rows = jnp.concatenate([keep_ref[...].astype(F32), recv_ref[...].astype(F32)], axis=0)
    out_ref[...] = jnp.dot(
        selector.astype(BF16), rows.astype(BF16), preferred_element_type=F32
    ).astype(BF16)


def swap(array, axis, bit):
    return lax.ppermute(array, axis, [(i, i ^ bit) for i in range(lax.axis_size(axis))])


def per_device(x_rows, dy_rows, w_in, w_out, counts, assign):
    slots, width = x_rows.shape
    hidden_units = w_out.shape[2]
    groups = lax.axis_size("dp")
    units = lax.axis_size("expert")
    parts = lax.axis_size("mp")
    owners = counts.shape[1]
    capacity = slots // owners
    quarter = width // groups
    share = width // parts
    dp_bits, unit_bits, part_bits = bits_of(groups), bits_of(units), bits_of(parts)

    split = pl.pallas_call(
        functools.partial(split_kernel, dp_bits),
        out_shape=[shape((2 * slots, width // 2 ** (i + 1))) for i in range(dp_bits)]
        + [shape((2 * slots, quarter))],
        in_specs=[IN_HBM, IN_HBM],
        out_specs=[ANY] * (dp_bits + 1),
        scratch_shapes=[pltpu.SemaphoreType.DMA((2 * dp_bits + 2,))],
        compiler_params=params(),
        cost_estimate=pl.CostEstimate(flops=0, bytes_accessed=2**19, transcendentals=0),
        name="split_rows",
    )(x_rows, dy_rows)
    sent = [split[dp_bits], swap(split[0], "dp", groups // 2)]

    w_flat = jnp.transpose(w_in[0], (1, 2, 0)).reshape(2 * hidden_units, width)
    w_down = jnp.transpose(w_out[0], (1, 0))
    copies = 3 + len(cuts_of(2 * hidden_units)) + len(cuts_of(hidden_units))
    acts, keep, send = pl.pallas_call(
        functools.partial(acts_kernel, parts),
        out_shape=[
            shape((slots, 3 * hidden_units)),
            shape((slots, width // 2), F32),
            shape((slots, width // 2)),
        ],
        in_specs=[IN_HBM] * 5,
        out_specs=[IN_VMEM] * 3,
        scratch_shapes=[
            pltpu.VMEM(x_rows.shape, BF16),
            pltpu.VMEM(dy_rows.shape, BF16),
            pltpu.VMEM(w_flat.shape, BF16),
            pltpu.VMEM(w_down.shape, BF16),
            pltpu.SMEM(counts.shape, jnp.int32),
            pltpu.VMEM((slots, width), F32),
            pltpu.SemaphoreType.DMA((copies,)),
        ],
        compiler_params=params(),
        cost_estimate=pl.CostEstimate(
            flops=2 * 256 * width * 5 * hidden_units,
            bytes_accessed=6 * hidden_units * width,
            transcendentals=0,
        ),
        name="acts_and_rows",
    )(x_rows, dy_rows, w_flat, w_down, counts)

    acts_all = [acts]
    swaps = [("mp", parts >> (i + 1)) for i in range(part_bits)]
    swaps += [("expert", units >> (i + 1)) for i in range(unit_bits)]
    rows_held = slots
    for step in range(max(len(swaps), dp_bits)):
        tasks = []
        if step > 0:
            if step < len(swaps):
                if step < part_bits:
                    body = sum_task(part_bits, step - 1, width)
                    out = (slots, width >> (step + 1))
                elif step == part_bits:
                    body = sum_task(part_bits, step - 1, width)
                    out = (slots // 2, share)
                else:
                    past = step - part_bits
                    body = deal_task(owners >> past, capacity << (past - 1))
                    out = (slots // 2, share)
                tasks.append((body, [keep, recv], [shape(out, F32), shape(out)]))
            if step < dp_bits:
                tasks.append((stack_task, acts_all, [shape((slots << step, 3 * hidden_units))]))
                tasks.append(
                    (
                        columns_task(dp_bits, step, width),
                        [split[step]] + sent[1:],
                        [shape((2 * slots << step, width >> (step + 1)))],
                    )
                )
            results = run_tasks(tasks, "merge%d" % step)
            if step < len(swaps):
                keep, send = results[0]
        if step < len(swaps):
            recv = swap(send, *swaps[step])
        if step < dp_bits:
            bit = groups >> (step + 1)
            acts_all.append(swap(acts if step == 0 else results[-2][0], "dp", bit))
            if step > 0:
                sent.append(swap(results[-1][0], "dp", bit))

    grad_in, grad_out = pl.pallas_call(
        functools.partial(weights_kernel, dp_bits, width),
        out_shape=[shape((2 * hidden_units, quarter)), shape((hidden_units, quarter))],
        in_specs=[IN_VMEM] * (2 + 2 * dp_bits),
        out_specs=[ANY, ANY],
        scratch_shapes=[
            pltpu.VMEM((2 * hidden_units, quarter), BF16),
            pltpu.VMEM((hidden_units, quarter), BF16),
            pltpu.SemaphoreType.DMA((len(cuts_of(2 * hidden_units)) + len(cuts_of(hidden_units)),)),
        ],
        compiler_params=params(),
        cost_estimate=pl.CostEstimate(
            flops=2 * 256 * quarter * 3 * hidden_units,
            bytes_accessed=6 * hidden_units * quarter,
            transcendentals=0,
        ),
        name="weight_grads",
    )(*sent, *acts_all)

    grad_tokens = pl.pallas_call(
        functools.partial(tokens_kernel, units, capacity),
        out_shape=shape((assign.shape[0], share)),
        in_specs=[IN_SMEM, IN_VMEM, IN_VMEM],
        out_specs=IN_VMEM,
        compiler_params=params(),
        name="token_grads",
    )(assign.T, keep, recv)

    grad_w_in = grad_in.reshape(2, hidden_units, quarter).transpose(2, 0, 1)[None]
    grad_w_out = grad_out.transpose(1, 0)[None]
    return (grad_w_in, grad_w_out, grad_tokens)


def solution(mesh):
    return jax.shard_map(
        per_device,
        mesh=mesh,
        in_specs=(
            P(("dp", "expert"), None),
            P(("dp", "expert"), None),
            P("expert", None, None, "mp"),
            P("expert", None, "mp"),
            P(("dp", "expert"), None),
            P(("dp", "expert"), None),
        ),
        out_specs=(
            P("expert", "dp", None, "mp"),
            P("expert", "dp", "mp"),
            P(("dp", "expert"), "mp"),
        ),
        check_vma=False,
    )
```

```python
import functools

import jax
import jax.numpy as jnp
from jax import lax
from jax.experimental import pallas as pl
from jax.experimental.pallas import tpu as pltpu
from jax.sharding import PartitionSpec as P

LAYER_EXPERTS = 16
BF16 = jnp.bfloat16
F32 = jnp.float32
VMEM_BYTES = 48 * 1024 * 1024
CONTRACT_LAST = (((1,), (1,)), ((), ()))

ANY = pl.BlockSpec(memory_space=pl.ANY)
IN_HBM = pl.BlockSpec(memory_space=pltpu.HBM)
IN_VMEM = pl.BlockSpec(memory_space=pltpu.VMEM)


def shape(dims, dtype=BF16):
    return jax.ShapeDtypeStruct(dims, dtype)


def params():
    return pltpu.CompilerParams(vmem_limit_bytes=VMEM_BYTES)


def bits_of(size):
    return size.bit_length() - 1


def cuts_of(rows, most=256, unit=16):
    pieces = -(-rows // most)
    size = -(-rows // pieces)
    size = -(-size // unit) * unit
    return [(at, min(size, rows - at)) for at in range(0, rows, size)]


def column_start(me, bits, step, width, flipped):
    place = lax.shift_right_logical(me, jnp.int32(bits - 1 - step))
    if flipped:
        place = place ^ 1
    return place * (width // 2 ** (step + 1))


def lanes(start, size):
    return pl.ds(pl.multiple_of(start, 128), size)


def split_kernel(bits, x_ref, dy_ref, *rest):
    outs, sems = rest[: bits + 1], rest[bits + 1]
    rows, width = x_ref.shape
    me = lax.axis_index("dp")
    copies = []
    for step in range(bits + 1):
        own = step == bits
        last = min(step, bits - 1)
        start = column_start(me, bits, last, width, not own)
        size = width // 2 ** (last + 1)
        for half, ref in enumerate((x_ref, dy_ref)):
            copy = pltpu.make_async_copy(
                ref.at[:, lanes(start, size)],
                outs[step].at[pl.ds(half * rows, rows), :],
                sems.at[2 * step + half],
            )
            copy.start()
            copies.append(copy)
    for copy in copies:
        copy.wait()


def pick_matrix(counts_ref, slots, my_unit):
    owners = counts_ref.shape[1]
    capacity = slots // owners
    row_at = lax.broadcasted_iota(jnp.int32, (slots, slots), 0)
    slot_at = lax.broadcasted_iota(jnp.int32, (slots, slots), 1)
    pick = jnp.zeros((slots, slots), F32)
    total = jnp.int32(0)
    for owner in range(owners):
        held = counts_ref[0, owner]
        first = (my_unit ^ owner) * capacity
        hit = (row_at >= first) & (row_at < first + held) & (slot_at - row_at == total - first)
        pick = jnp.where(hit, 1.0, pick)
        total = total + held
    return pick


def token_selector(assign_ref, units, capacity, my_unit):
    bits = bits_of(units)
    width, tokens = assign_ref.shape
    slices = units // min(LAYER_EXPERTS, units)
    dims = (tokens, units * capacity)
    token_at = lax.broadcasted_iota(jnp.int32, dims, 0)
    column_at = lax.broadcasted_iota(jnp.int32, dims, 1)
    selector = jnp.zeros(dims, F32)
    for token in range(tokens):
        for k in range(width):
            expert = assign_ref[k, token]
            rank = jnp.int32(0)
            for earlier in range(token):
                for other in range(width):
                    rank = rank + (assign_ref[other, earlier] == expert).astype(jnp.int32)
            for piece in range(slices):
                apart = (expert * slices + piece) ^ my_unit
                place = jnp.int32(0)
                for bit in range(bits):
                    place = place * 2 + (lax.shift_right_logical(apart, jnp.int32(bit)) & 1)
                hit = (token_at == token) & (column_at == place * capacity + rank)
                selector = jnp.where(hit, selector + 1.0, selector)
    return selector


def acts_kernel(units, parts, *refs):
    x_hbm, dy_hbm, w_in_hbm, w_out_hbm, counts_hbm, assign_hbm = refs[:6]
    acts_ref, keep_ref, send_ref, selector_ref = refs[6:10]
    x_ref, dy_ref, w_in_ref, w_out_ref, counts_ref, assign_ref, rows_ref, sems = refs[10:]

    hidden_units, width = w_out_ref.shape
    cuts = cuts_of(hidden_units, 128)
    plan = [(counts_hbm, counts_ref), (x_hbm, x_ref), (dy_hbm, dy_ref)]
    for at, size in cuts:
        for half in range(2):
            plan.append(
                (
                    w_in_hbm.at[pl.ds(half * hidden_units + at, size), :],
                    w_in_ref.at[pl.ds(2 * at + half * size, size), :],
                )
            )
        plan.append((w_out_hbm.at[pl.ds(at, size), :], w_out_ref.at[pl.ds(at, size), :]))
    plan.append((assign_hbm, assign_ref))
    copies = [pltpu.make_async_copy(s, d, sems.at[i]) for i, (s, d) in enumerate(plan)]
    for copy in copies:
        copy.start()
    copies = iter(copies)

    slots = x_ref.shape[0]
    capacity = slots // counts_ref.shape[1]
    my_unit = lax.axis_index("expert")
    next(copies).wait()
    pick = pick_matrix(counts_ref, slots, my_unit)
    back = pick.T.astype(BF16)
    pick = pick.astype(BF16)
    next(copies).wait()
    x = jnp.dot(pick, x_ref[...], preferred_element_type=F32).astype(BF16)
    next(copies).wait()
    dy = jnp.dot(pick, dy_ref[...], preferred_element_type=F32).astype(BF16)

    gates, ups, hiddens = [], [], []
    for at, size in cuts:
        next(copies).wait()
        next(copies).wait()
        w_both = w_in_ref.at[pl.ds(2 * at, 2 * size), :]
        pre = lax.dot_general(x, w_both[...], CONTRACT_LAST, preferred_element_type=F32)
        next(copies).wait()
        grad_hidden = lax.dot_general(
            dy, w_out_ref[pl.ds(at, size), :], CONTRACT_LAST, preferred_element_type=F32
        )
        gate_pre, up_pre = pre[:, :size], pre[:, size:]
        sigmoid_gate = jax.nn.sigmoid(gate_pre)
        hidden = gate_pre * sigmoid_gate * up_pre
        grad_gate = grad_hidden * up_pre * sigmoid_gate * (1.0 + gate_pre * (1.0 - sigmoid_gate))
        grad_up = grad_hidden * gate_pre * sigmoid_gate
        grad_pre = jnp.concatenate([grad_gate, grad_up], axis=1).astype(BF16)
        for left, count in cuts_of(width, 1024, 128):
            here = pl.ds(left, count)
            part = jnp.dot(grad_pre, w_both[:, here], preferred_element_type=F32)
            if at:
                part = part + rows_ref[:, here]
            rows_ref[:, here] = part
        gates.append(grad_gate)
        ups.append(grad_up)
        hiddens.append(hidden)
    acts = jnp.concatenate(gates + ups + hiddens, axis=1).astype(BF16)
    acts_ref[...] = jnp.dot(back, acts, preferred_element_type=F32).astype(BF16)

    my_part = lax.axis_index("mp")
    bits = bits_of(parts)
    keep_ref[...] = rows_ref[:, lanes(column_start(my_part, bits, 0, width, False), width // 2)]
    send_ref[...] = rows_ref[
        :, lanes(column_start(my_part, bits, 0, width, True), width // 2)
    ].astype(BF16)
    next(copies).wait()
    selector_ref[...] = token_selector(assign_ref, units, capacity, my_unit)


def sum_task(bits, step, width):
    def body(ins, outs):
        keep_ref, recv_ref = ins
        total = keep_ref[...].astype(F32) + recv_ref[...].astype(F32)
        if step + 1 < bits:
            me = lax.axis_index("mp")
            base = column_start(me, bits, step, width, False)
            size = width // 2 ** (step + 2)
            is_high = column_start(me, bits, step + 1, width, False) - base > 0
            low, high = total[:, :size], total[:, size:]
            outs[0][...] = jnp.where(is_high, high, low)
            outs[1][...] = jnp.where(is_high, low, high).astype(BF16)
        else:
            half = total.shape[0] // 2
            outs[0][...] = total[:half]
            outs[1][...] = total[half:].astype(BF16)

    return body


def deal_task(blocks, block):
    def body(ins, outs):
        keep, recv = ins[0][...].astype(F32), ins[1][...].astype(F32)
        joined = []
        for at in range(blocks):
            joined += [keep[at * block : (at + 1) * block], recv[at * block : (at + 1) * block]]
        outs[0][...] = jnp.concatenate(joined[:blocks], axis=0)
        outs[1][...] = jnp.concatenate(joined[blocks:], axis=0).astype(BF16)

    return body


def stack_task(ins, outs):
    at = 0
    for ref in ins:
        outs[0][pl.ds(at, ref.shape[0]), :] = ref[...]
        at += ref.shape[0]


def columns_task(bits, step, width):
    def body(ins, outs):
        me = lax.axis_index("dp")
        size = width // 2 ** (step + 1)
        start = column_start(me, bits, step, width, True)
        rows = ins[0].shape[0]
        outs[0][pl.ds(0, rows), :] = ins[0][...]
        at = rows
        for past, ref in enumerate(ins[1:]):
            base = column_start(me, bits, past, width, False)
            outs[0][pl.ds(at, ref.shape[0]), :] = ref[:, lanes(start - base, size)]
            at += ref.shape[0]

    return body


def run_tasks(tasks, name):
    ins = [array for _, arrays, _ in tasks for array in arrays]
    outs = [out for _, _, out_shapes in tasks for out in out_shapes]

    def kernel(*refs):
        in_at, out_at = 0, len(ins)
        for body, arrays, out_shapes in tasks:
            body(
                refs[in_at : in_at + len(arrays)],
                refs[out_at : out_at + len(out_shapes)],
            )
            in_at += len(arrays)
            out_at += len(out_shapes)

    results = iter(
        pl.pallas_call(
            kernel,
            out_shape=outs,
            in_specs=[IN_VMEM] * len(ins),
            out_specs=[IN_VMEM] * len(outs),
            compiler_params=params(),
            name=name,
        )(*ins)
    )
    return [[next(results) for _ in out_shapes] for _, _, out_shapes in tasks]


def weights_kernel(bits, width, *refs):
    count = 1 + bits
    sent, acts = refs[:count], refs[count : 2 * count]
    in_hbm, out_hbm, in_ref, out_ref, sems = refs[2 * count :]
    slots = acts[0].shape[0]
    me = lax.axis_index("dp")
    quarter = width // 2**bits
    x, dy = [], []
    for index, ref in enumerate(sent):
        if index == 0:
            block = ref[...]
        else:
            base = column_start(me, bits, index - 1, width, False)
            block = ref[:, lanes(me * quarter - base, quarter)]
        for at in range(0, block.shape[0], 2 * slots):
            x.append(block[at : at + slots])
            dy.append(block[at + slots : at + 2 * slots])
    x, dy = jnp.concatenate(x, axis=0), jnp.concatenate(dy, axis=0)
    columns = jnp.concatenate([ref[...] for ref in acts], axis=0).T
    copies = []
    start = 0
    for values, target, staged in ((x, in_hbm, in_ref), (dy, out_hbm, out_ref)):
        for at, size in cuts_of(target.shape[0]):
            here = pl.ds(at, size)
            staged[here, :] = jnp.dot(
                columns[start + at : start + at + size], values, preferred_element_type=F32
            ).astype(BF16)
            copy = pltpu.make_async_copy(
                staged.at[here, :], target.at[here, :], sems.at[len(copies)]
            )
            copy.start()
            copies.append(copy)
        start += target.shape[0]
    for copy in copies:
        copy.wait()


def tokens_kernel(selector_ref, keep_ref, recv_ref, out_ref):
    rows = jnp.concatenate([keep_ref[...].astype(F32), recv_ref[...].astype(F32)], axis=0)
    out_ref[...] = jnp.dot(
        selector_ref[...].astype(BF16), rows.astype(BF16), preferred_element_type=F32
    ).astype(BF16)


def in_hbm(array):
    return pltpu.with_memory_space_constraint(array, pltpu.HBM)


def swap(array, axis, bit):
    return lax.ppermute(array, axis, [(i, i ^ bit) for i in range(lax.axis_size(axis))])


def per_device(x_rows, dy_rows, w_in, w_out, counts, assign):
    slots, width = x_rows.shape
    hidden_units = w_out.shape[2]
    groups = lax.axis_size("dp")
    units = lax.axis_size("expert")
    parts = lax.axis_size("mp")
    owners = counts.shape[1]
    capacity = slots // owners
    quarter = width // groups
    share = width // parts
    dp_bits, unit_bits, part_bits = bits_of(groups), bits_of(units), bits_of(parts)

    split = pl.pallas_call(
        functools.partial(split_kernel, dp_bits),
        out_shape=[shape((2 * slots, width // 2 ** (i + 1))) for i in range(dp_bits)]
        + [shape((2 * slots, quarter))],
        in_specs=[IN_HBM, IN_HBM],
        out_specs=[ANY] * (dp_bits + 1),
        scratch_shapes=[pltpu.SemaphoreType.DMA((2 * dp_bits + 2,))],
        compiler_params=params(),
        cost_estimate=pl.CostEstimate(flops=0, bytes_accessed=2**19, transcendentals=0),
        name="split_rows",
    )(in_hbm(x_rows), in_hbm(dy_rows))
    sent = [split[dp_bits], swap(split[0], "dp", groups // 2)]

    w_flat = jnp.transpose(w_in[0], (1, 2, 0)).reshape(2 * hidden_units, width)
    w_down = jnp.transpose(w_out[0], (1, 0))
    copies = 4 + 3 * len(cuts_of(hidden_units, 128))
    acts, keep, send, selector = pl.pallas_call(
        functools.partial(acts_kernel, units, parts),
        out_shape=[
            shape((slots, 3 * hidden_units)),
            shape((slots, width // 2), F32),
            shape((slots, width // 2)),
            shape((assign.shape[0], slots), F32),
        ],
        in_specs=[IN_HBM] * 6,
        out_specs=[IN_VMEM] * 4,
        scratch_shapes=[
            pltpu.VMEM(x_rows.shape, BF16),
            pltpu.VMEM(dy_rows.shape, BF16),
            pltpu.VMEM(w_flat.shape, BF16),
            pltpu.VMEM(w_down.shape, BF16),
            pltpu.SMEM(counts.shape, jnp.int32),
            pltpu.SMEM(assign.shape[::-1], jnp.int32),
            pltpu.VMEM((slots, width), F32),
            pltpu.SemaphoreType.DMA((copies,)),
        ],
        compiler_params=params(),
        cost_estimate=pl.CostEstimate(
            flops=2 * 256 * width * 5 * hidden_units,
            bytes_accessed=6 * hidden_units * width,
            transcendentals=0,
        ),
        name="acts_and_rows",
    )(*map(in_hbm, (x_rows, dy_rows, w_flat, w_down, counts, assign.T)))

    acts_all = [acts]
    swaps = [("mp", parts >> (i + 1)) for i in range(part_bits)]
    swaps += [("expert", units >> (i + 1)) for i in range(unit_bits)]
    rows_held = slots
    for step in range(max(len(swaps), dp_bits)):
        tasks = []
        if step > 0:
            if step < len(swaps):
                if step < part_bits:
                    body = sum_task(part_bits, step - 1, width)
                    out = (slots, width >> (step + 1))
                elif step == part_bits:
                    body = sum_task(part_bits, step - 1, width)
                    out = (slots // 2, share)
                else:
                    past = step - part_bits
                    body = deal_task(owners >> past, capacity << (past - 1))
                    out = (slots // 2, share)
                tasks.append((body, [keep, recv], [shape(out, F32), shape(out)]))
            if step < dp_bits:
                tasks.append((stack_task, acts_all, [shape((slots << step, 3 * hidden_units))]))
                tasks.append(
                    (
                        columns_task(dp_bits, step, width),
                        [split[step]] + sent[1:],
                        [shape((2 * slots << step, width >> (step + 1)))],
                    )
                )
            names = ["rows%d", "acts%d", "columns%d"][-len(tasks) :] if step < dp_bits else ["rows%d"]
            results = [run_tasks([t], n % step)[0] for t, n in zip(tasks, names)]
            if step < len(swaps):
                keep, send = results[0]
        if step < len(swaps):
            recv = swap(send, *swaps[step])
        if step < dp_bits:
            bit = groups >> (step + 1)
            acts_all.append(swap(acts if step == 0 else results[-2][0], "dp", bit))
            if step > 0:
                sent.append(swap(results[-1][0], "dp", bit))

    grad_in, grad_out = pl.pallas_call(
        functools.partial(weights_kernel, dp_bits, width),
        out_shape=[shape((2 * hidden_units, quarter)), shape((hidden_units, quarter))],
        in_specs=[IN_VMEM] * (2 + 2 * dp_bits),
        out_specs=[ANY, ANY],
        scratch_shapes=[
            pltpu.VMEM((2 * hidden_units, quarter), BF16),
            pltpu.VMEM((hidden_units, quarter), BF16),
            pltpu.SemaphoreType.DMA((len(cuts_of(2 * hidden_units)) + len(cuts_of(hidden_units)),)),
        ],
        compiler_params=params(),
        cost_estimate=pl.CostEstimate(
            flops=2 * 256 * quarter * 3 * hidden_units,
            bytes_accessed=6 * hidden_units * quarter,
            transcendentals=0,
        ),
        name="weight_grads",
    )(*sent, *acts_all)

    grad_tokens = pl.pallas_call(
        tokens_kernel,
        out_shape=shape((assign.shape[0], share)),
        in_specs=[IN_VMEM] * 3,
        out_specs=IN_VMEM,
        compiler_params=params(),
        name="token_grads",
    )(selector, keep, recv)

    grad_w_in = grad_in.reshape(2, hidden_units, quarter).transpose(2, 0, 1)[None]
    grad_w_out = grad_out.transpose(1, 0)[None]
    return (grad_w_in, grad_w_out, grad_tokens)


def solution(mesh):
    return jax.shard_map(
        per_device,
        mesh=mesh,
        in_specs=(
            P(("dp", "expert"), None),
            P(("dp", "expert"), None),
            P("expert", None, None, "mp"),
            P("expert", None, "mp"),
            P(("dp", "expert"), None),
            P(("dp", "expert"), None),
        ),
        out_specs=(
            P("expert", "dp", None, "mp"),
            P("expert", "dp", "mp"),
            P(("dp", "expert"), "mp"),
        ),
        check_vma=False,
    )
```

```python
import functools

import jax
import jax.numpy as jnp
from jax import lax
from jax.experimental import pallas as pl
from jax.experimental.pallas import tpu as pltpu
from jax.sharding import PartitionSpec as P

LAYER_EXPERTS = 16
BF16 = jnp.bfloat16
F32 = jnp.float32
VMEM_BYTES = 48 * 1024 * 1024
CONTRACT_LAST = (((1,), (1,)), ((), ()))

ANY = pl.BlockSpec(memory_space=pl.ANY)
IN_HBM = pl.BlockSpec(memory_space=pltpu.HBM)
IN_VMEM = pl.BlockSpec(memory_space=pltpu.VMEM)


def shape(dims, dtype=BF16):
    return jax.ShapeDtypeStruct(dims, dtype)


def params():
    return pltpu.CompilerParams(vmem_limit_bytes=VMEM_BYTES)


def bits_of(size):
    return size.bit_length() - 1


def cuts_of(rows, most=256, unit=16):
    pieces = -(-rows // most)
    size = -(-rows // pieces)
    size = -(-size // unit) * unit
    return [(at, min(size, rows - at)) for at in range(0, rows, size)]


def column_start(me, bits, step, width, flipped):
    place = lax.shift_right_logical(me, jnp.int32(bits - 1 - step))
    if flipped:
        place = place ^ 1
    return place * (width // 2 ** (step + 1))


def lanes(start, size):
    return pl.ds(pl.multiple_of(start, 128), size)


def split_kernel(bits, x_ref, dy_ref, *rest):
    outs, sems = rest[: bits + 1], rest[bits + 1]
    rows, width = x_ref.shape
    me = lax.axis_index("dp")
    copies = []
    for step in range(bits + 1):
        own = step == bits
        last = min(step, bits - 1)
        start = column_start(me, bits, last, width, not own)
        size = width // 2 ** (last + 1)
        for half, ref in enumerate((x_ref, dy_ref)):
            copy = pltpu.make_async_copy(
                ref.at[:, lanes(start, size)],
                outs[step].at[pl.ds(half * rows, rows), :],
                sems.at[2 * step + half],
            )
            copy.start()
            copies.append(copy)
    for copy in copies:
        copy.wait()


def pick_matrix(counts_ref, slots, my_unit):
    owners = counts_ref.shape[1]
    capacity = slots // owners
    row_at = lax.broadcasted_iota(jnp.int32, (slots, slots), 0)
    slot_at = lax.broadcasted_iota(jnp.int32, (slots, slots), 1)
    pick = jnp.zeros((slots, slots), F32)
    total = jnp.int32(0)
    for owner in range(owners):
        held = counts_ref[0, owner]
        first = (my_unit ^ owner) * capacity
        hit = (row_at >= first) & (row_at < first + held) & (slot_at - row_at == total - first)
        pick = jnp.where(hit, 1.0, pick)
        total = total + held
    return pick


def token_selector(assign_ref, units, capacity, my_unit):
    bits = bits_of(units)
    width, tokens = assign_ref.shape
    slices = units // min(LAYER_EXPERTS, units)
    dims = (tokens, units * capacity)
    token_at = lax.broadcasted_iota(jnp.int32, dims, 0)
    column_at = lax.broadcasted_iota(jnp.int32, dims, 1)
    selector = jnp.zeros(dims, F32)
    for token in range(tokens):
        for k in range(width):
            expert = assign_ref[k, token]
            rank = jnp.int32(0)
            for earlier in range(token):
                for other in range(width):
                    rank = rank + (assign_ref[other, earlier] == expert).astype(jnp.int32)
            for piece in range(slices):
                apart = (expert * slices + piece) ^ my_unit
                place = jnp.int32(0)
                for bit in range(bits):
                    place = place * 2 + (lax.shift_right_logical(apart, jnp.int32(bit)) & 1)
                hit = (token_at == token) & (column_at == place * capacity + rank)
                selector = jnp.where(hit, selector + 1.0, selector)
    return selector


def unit_cuts(hidden_units):
    cuts = [(at, min(128, hidden_units - at)) for at in range(0, hidden_units, 128)]
    runs = [cuts[:1]] + [cuts[i : i + 2] for i in range(1, len(cuts), 2)]
    return cuts, runs


def acts_kernel(units, parts, *refs):
    x_hbm, dy_hbm, w_in_hbm, w_out_hbm, counts_hbm, assign_hbm = refs[:6]
    acts_ref, keep_ref, send_ref, selector_ref = refs[6:10]
    x_ref, dy_ref, w_in_ref, w_out_ref, counts_ref, assign_ref, rows_ref, sems = refs[10:]

    hidden_units, width = w_out_ref.shape
    cuts, runs = unit_cuts(hidden_units)
    used = []

    def begin(source, target):
        copy = pltpu.make_async_copy(source, target, sems.at[len(used)])
        copy.start()
        used.append(copy)
        return copy

    counts_copy = begin(counts_hbm, counts_ref)
    x_copy = begin(x_hbm, x_ref)
    in_copies, out_copies = [], []
    dy_copy = None
    for run in runs:
        for at, size in run:
            in_copies.append(
                [
                    begin(
                        w_in_hbm.at[pl.ds(half * hidden_units + at, size), :],
                        w_in_ref.at[pl.ds(2 * at + half * size, size), :],
                    )
                    for half in range(2)
                ]
            )
            if at == run[0][0]:
                if dy_copy is None:
                    dy_copy = begin(dy_hbm, dy_ref)
                here = pl.ds(at, sum(n for _, n in run))
                out_copies.append(begin(w_out_hbm.at[here, :], w_out_ref.at[here, :]))
    assign_copy = begin(assign_hbm, assign_ref)

    slots = x_ref.shape[0]
    capacity = slots // counts_ref.shape[1]
    my_unit = lax.axis_index("expert")
    counts_copy.wait()
    pick = pick_matrix(counts_ref, slots, my_unit)
    back = pick.T.astype(BF16)
    pick = pick.astype(BF16)
    x_copy.wait()
    x = jnp.dot(pick, x_ref[...], preferred_element_type=F32).astype(BF16)
    dy = None

    gates, ups, hiddens = [], [], []

    def add_rows(at, size, pre, grad_hidden):
        gate_pre, up_pre = pre[:, :size], pre[:, size:]
        sigmoid_gate = jax.nn.sigmoid(gate_pre)
        hidden = gate_pre * sigmoid_gate * up_pre
        grad_gate = grad_hidden * up_pre * sigmoid_gate * (1.0 + gate_pre * (1.0 - sigmoid_gate))
        grad_up = grad_hidden * gate_pre * sigmoid_gate
        grad_pre = jnp.concatenate([grad_gate, grad_up], axis=1).astype(BF16)
        gates.append(grad_gate)
        ups.append(grad_up)
        hiddens.append(hidden)
        for left, count in cuts_of(width, 1024, 128):
            here = pl.ds(left, count)
            part = jnp.dot(
                grad_pre, w_in_ref[pl.ds(2 * at, 2 * size), here], preferred_element_type=F32
            )
            if at:
                part = part + rows_ref[:, here]
            rows_ref[:, here] = part

    waiting = None
    for run, out_copy in zip(runs, out_copies):
        grad_hidden = None
        for at, size in run:
            for copy in in_copies.pop(0):
                copy.wait()
            pre = lax.dot_general(
                x,
                w_in_ref[pl.ds(2 * at, 2 * size), :],
                CONTRACT_LAST,
                preferred_element_type=F32,
            )
            if grad_hidden is None:
                if dy is None:
                    dy_copy.wait()
                    dy = jnp.dot(pick, dy_ref[...], preferred_element_type=F32).astype(BF16)
                out_copy.wait()
                start, total = at, sum(n for _, n in run)
                grad_hidden = lax.dot_general(
                    dy,
                    w_out_ref[pl.ds(start, total), :],
                    CONTRACT_LAST,
                    preferred_element_type=F32,
                )
            if waiting is not None:
                add_rows(*waiting)
            waiting = (at, size, pre, grad_hidden[:, at - start : at - start + size])
    add_rows(*waiting)
    acts = jnp.concatenate(gates + ups + hiddens, axis=1).astype(BF16)
    acts_ref[...] = jnp.dot(back, acts, preferred_element_type=F32).astype(BF16)

    my_part = lax.axis_index("mp")
    bits = bits_of(parts)
    keep_ref[...] = rows_ref[:, lanes(column_start(my_part, bits, 0, width, False), width // 2)]
    send_ref[...] = rows_ref[
        :, lanes(column_start(my_part, bits, 0, width, True), width // 2)
    ].astype(BF16)
    assign_copy.wait()
    selector_ref[...] = token_selector(assign_ref, units, capacity, my_unit)


def sum_task(bits, step, width):
    def body(ins, outs):
        keep_ref, recv_ref = ins
        total = keep_ref[...].astype(F32) + recv_ref[...].astype(F32)
        if step + 1 < bits:
            me = lax.axis_index("mp")
            base = column_start(me, bits, step, width, False)
            size = width // 2 ** (step + 2)
            is_high = column_start(me, bits, step + 1, width, False) - base > 0
            low, high = total[:, :size], total[:, size:]
            outs[0][...] = jnp.where(is_high, high, low)
            outs[1][...] = jnp.where(is_high, low, high).astype(BF16)
        else:
            half = total.shape[0] // 2
            outs[0][...] = total[:half]
            outs[1][...] = total[half:].astype(BF16)

    return body


def deal_task(blocks, block):
    def body(ins, outs):
        keep, recv = ins[0][...].astype(F32), ins[1][...].astype(F32)
        joined = []
        for at in range(blocks):
            joined += [keep[at * block : (at + 1) * block], recv[at * block : (at + 1) * block]]
        outs[0][...] = jnp.concatenate(joined[:blocks], axis=0)
        outs[1][...] = jnp.concatenate(joined[blocks:], axis=0).astype(BF16)

    return body


def stack_task(ins, outs):
    at = 0
    for ref in ins:
        outs[0][pl.ds(at, ref.shape[0]), :] = ref[...]
        at += ref.shape[0]


def columns_task(bits, step, width):
    def body(ins, outs):
        me = lax.axis_index("dp")
        size = width // 2 ** (step + 1)
        start = column_start(me, bits, step, width, True)
        rows = ins[0].shape[0]
        outs[0][pl.ds(0, rows), :] = ins[0][...]
        at = rows
        for past, ref in enumerate(ins[1:]):
            base = column_start(me, bits, past, width, False)
            outs[0][pl.ds(at, ref.shape[0]), :] = ref[:, lanes(start - base, size)]
            at += ref.shape[0]

    return body


def run_whole(body, ins, outs, name, after=None):
    extra = [] if after is None else [after]

    def kernel(*refs):
        body(refs[: len(ins)], refs[len(ins) + len(extra) :])

    return pl.pallas_call(
        kernel,
        out_shape=outs,
        in_specs=[IN_VMEM] * (len(ins) + len(extra)),
        out_specs=[IN_VMEM] * len(outs),
        compiler_params=params(),
        name=name,
    )(*ins, *extra)


def weights_kernel(bits, width, *refs):
    count = 1 + bits
    sent, acts = refs[:count], refs[count : 2 * count]
    selector_ref, keep_ref, recv_ref = refs[2 * count : 2 * count + 3]
    in_hbm, out_hbm, tokens_hbm, in_ref, out_ref, tokens_ref, sems = refs[2 * count + 3 :]
    slots = acts[0].shape[0]
    me = lax.axis_index("dp")
    quarter = width // 2**bits
    x, dy = [], []
    for index, ref in enumerate(sent):
        if index == 0:
            block = ref[...]
        else:
            base = column_start(me, bits, index - 1, width, False)
            block = ref[:, lanes(me * quarter - base, quarter)]
        for at in range(0, block.shape[0], 2 * slots):
            x.append(block[at : at + slots])
            dy.append(block[at + slots : at + 2 * slots])
    x, dy = jnp.concatenate(x, axis=0), jnp.concatenate(dy, axis=0)
    columns = jnp.concatenate([ref[...] for ref in acts], axis=0).T
    copies = []

    def begin(source, target):
        copy = pltpu.make_async_copy(source, target, sems.at[len(copies)])
        copy.start()
        copies.append(copy)

    start = 0
    for values, target, staged in ((x, in_hbm, in_ref), (dy, out_hbm, out_ref)):
        for at, size in cuts_of(target.shape[0]):
            here = pl.ds(at, size)
            staged[here, :] = jnp.dot(
                columns[start + at : start + at + size], values, preferred_element_type=F32
            ).astype(BF16)
            begin(staged.at[here, :], target.at[here, :])
        start += target.shape[0]
    rows = jnp.concatenate([keep_ref[...].astype(F32), recv_ref[...].astype(F32)], axis=0)
    tokens_ref[...] = jnp.dot(
        selector_ref[...].astype(BF16), rows.astype(BF16), preferred_element_type=F32
    ).astype(BF16)
    begin(tokens_ref, tokens_hbm)
    for copy in copies:
        copy.wait()


def in_hbm(array):
    return pltpu.with_memory_space_constraint(array, pltpu.HBM)


def swap(array, axis, bit):
    return lax.ppermute(array, axis, [(i, i ^ bit) for i in range(lax.axis_size(axis))])


def per_device(x_rows, dy_rows, w_in, w_out, counts, assign):
    slots, width = x_rows.shape
    hidden_units = w_out.shape[2]
    groups = lax.axis_size("dp")
    units = lax.axis_size("expert")
    parts = lax.axis_size("mp")
    owners = counts.shape[1]
    capacity = slots // owners
    quarter = width // groups
    share = width // parts
    dp_bits, unit_bits, part_bits = bits_of(groups), bits_of(units), bits_of(parts)

    split = pl.pallas_call(
        functools.partial(split_kernel, dp_bits),
        out_shape=[shape((2 * slots, width // 2 ** (i + 1))) for i in range(dp_bits)]
        + [shape((2 * slots, quarter))],
        in_specs=[IN_HBM, IN_HBM],
        out_specs=[ANY] * (dp_bits + 1),
        scratch_shapes=[pltpu.SemaphoreType.DMA((2 * dp_bits + 2,))],
        compiler_params=params(),
        cost_estimate=pl.CostEstimate(flops=0, bytes_accessed=2**19, transcendentals=0),
        name="split_rows",
    )(in_hbm(x_rows), in_hbm(dy_rows))
    sent = [split[dp_bits], swap(split[0], "dp", groups // 2)]

    w_flat = jnp.transpose(w_in[0], (1, 2, 0)).reshape(2 * hidden_units, width)
    w_down = jnp.transpose(w_out[0], (1, 0))
    cuts, runs = unit_cuts(hidden_units)
    copies = 4 + 2 * len(cuts) + len(runs)
    acts, keep, send, selector = pl.pallas_call(
        functools.partial(acts_kernel, units, parts),
        out_shape=[
            shape((slots, 3 * hidden_units)),
            shape((slots, width // 2), F32),
            shape((slots, width // 2)),
            shape((assign.shape[0], slots), F32),
        ],
        in_specs=[IN_HBM] * 6,
        out_specs=[IN_VMEM] * 4,
        scratch_shapes=[
            pltpu.VMEM(x_rows.shape, BF16),
            pltpu.VMEM(dy_rows.shape, BF16),
            pltpu.VMEM(w_flat.shape, BF16),
            pltpu.VMEM(w_down.shape, BF16),
            pltpu.SMEM(counts.shape, jnp.int32),
            pltpu.SMEM(assign.shape[::-1], jnp.int32),
            pltpu.VMEM((slots, width), F32),
            pltpu.SemaphoreType.DMA((copies,)),
        ],
        compiler_params=params(),
        cost_estimate=pl.CostEstimate(
            flops=2 * 256 * width * 5 * hidden_units,
            bytes_accessed=6 * hidden_units * width,
            transcendentals=0,
        ),
        name="acts_and_rows",
    )(*map(in_hbm, (x_rows, dy_rows, w_flat, w_down, counts, assign.T)))

    acts_all = [acts]
    swaps = [("mp", parts >> (i + 1)) for i in range(part_bits)]
    swaps += [("expert", units >> (i + 1)) for i in range(unit_bits)]
    rows_held = slots
    for step in range(max(len(swaps), dp_bits)):
        if 0 < step < dp_bits:
            (columns,) = run_whole(
                columns_task(dp_bits, step, width),
                [split[step]] + sent[1:],
                [shape((2 * slots << step, width >> (step + 1)))],
                "columns%d" % step,
                after=recv,
            )
            sent.append(swap(columns, "dp", groups >> (step + 1)))
        if 0 < step < len(swaps):
            if step <= part_bits:
                body = sum_task(part_bits, step - 1, width)
                out = (slots, width >> (step + 1)) if step < part_bits else (slots // 2, share)
            else:
                past = step - part_bits
                body = deal_task(owners >> past, capacity << (past - 1))
                out = (slots // 2, share)
            keep, send = run_whole(body, [keep, recv], [shape(out, F32), shape(out)], "rows%d" % step)
        if step < len(swaps):
            recv = swap(send, *swaps[step])
        if step < dp_bits:
            held = acts
            if step > 0:
                (held,) = run_whole(
                    stack_task,
                    acts_all,
                    [shape((slots << step, 3 * hidden_units))],
                    "acts%d" % step,
                    after=keep,
                )
            acts_all.append(swap(held, "dp", groups >> (step + 1)))

    grad_in, grad_out, grad_tokens = pl.pallas_call(
        functools.partial(weights_kernel, dp_bits, width),
        out_shape=[
            shape((2 * hidden_units, quarter)),
            shape((hidden_units, quarter)),
            shape((assign.shape[0], share)),
        ],
        in_specs=[IN_VMEM] * (5 + 2 * dp_bits),
        out_specs=[ANY] * 3,
        scratch_shapes=[
            pltpu.VMEM((2 * hidden_units, quarter), BF16),
            pltpu.VMEM((hidden_units, quarter), BF16),
            pltpu.VMEM((assign.shape[0], share), BF16),
            pltpu.SemaphoreType.DMA(
                (1 + len(cuts_of(2 * hidden_units)) + len(cuts_of(hidden_units)),)
            ),
        ],
        compiler_params=params(),
        cost_estimate=pl.CostEstimate(
            flops=2 * 256 * quarter * 3 * hidden_units,
            bytes_accessed=6 * hidden_units * quarter,
            transcendentals=0,
        ),
        name="weight_and_token_grads",
    )(*sent, *acts_all, selector, keep, recv)

    grad_w_in = grad_in.reshape(2, hidden_units, quarter).transpose(2, 0, 1)[None]
    grad_w_out = grad_out.transpose(1, 0)[None]
    return (grad_w_in, grad_w_out, grad_tokens)


def solution(mesh):
    return jax.shard_map(
        per_device,
        mesh=mesh,
        in_specs=(
            P(("dp", "expert"), None),
            P(("dp", "expert"), None),
            P("expert", None, None, "mp"),
            P("expert", None, "mp"),
            P(("dp", "expert"), None),
            P(("dp", "expert"), None),
        ),
        out_specs=(
            P("expert", "dp", None, "mp"),
            P("expert", "dp", "mp"),
            P(("dp", "expert"), "mp"),
        ),
        check_vma=False,
    )
```

```python
import functools

import jax
import jax.numpy as jnp
from jax import lax
from jax.experimental import pallas as pl
from jax.experimental.pallas import tpu as pltpu
from jax.sharding import PartitionSpec as P

LAYER_EXPERTS = 16
BF16 = jnp.bfloat16
F32 = jnp.float32
VMEM_BYTES = 48 * 1024 * 1024
CONTRACT_LAST = (((1,), (1,)), ((), ()))

ANY = pl.BlockSpec(memory_space=pl.ANY)
IN_HBM = pl.BlockSpec(memory_space=pltpu.HBM)
IN_VMEM = pl.BlockSpec(memory_space=pltpu.VMEM)


def shape(dims, dtype=BF16):
    return jax.ShapeDtypeStruct(dims, dtype)


def params():
    return pltpu.CompilerParams(vmem_limit_bytes=VMEM_BYTES)


def bits_of(size):
    return size.bit_length() - 1


def cuts_of(rows, most=256, unit=16):
    pieces = -(-rows // most)
    size = -(-rows // pieces)
    size = -(-size // unit) * unit
    return [(at, min(size, rows - at)) for at in range(0, rows, size)]


def step_cuts(rows):
    return [(at, min(256, rows - at)) for at in range(0, rows, 256)]


def column_start(me, bits, step, width, flipped):
    place = lax.shift_right_logical(me, jnp.int32(bits - 1 - step))
    if flipped:
        place = place ^ 1
    return place * (width // 2 ** (step + 1))


def lanes(start, size):
    return pl.ds(pl.multiple_of(start, 128), size)


def split_kernel(bits, x_ref, dy_ref, *rest):
    outs, sems = rest[: bits + 1], rest[bits + 1]
    rows, width = x_ref.shape
    me = lax.axis_index("dp")
    copies = []
    for step in range(bits + 1):
        own = step == bits
        last = min(step, bits - 1)
        start = column_start(me, bits, last, width, not own)
        size = width // 2 ** (last + 1)
        for half, ref in enumerate((x_ref, dy_ref)):
            copy = pltpu.make_async_copy(
                ref.at[:, lanes(start, size)],
                outs[step].at[pl.ds(half * rows, rows), :],
                sems.at[2 * step + half],
            )
            copy.start()
            copies.append(copy)
    for copy in copies:
        copy.wait()


def pick_matrix(counts_ref, slots, my_unit):
    owners = counts_ref.shape[1]
    capacity = slots // owners
    row_at = lax.broadcasted_iota(jnp.int32, (slots, slots), 0)
    slot_at = lax.broadcasted_iota(jnp.int32, (slots, slots), 1)
    pick = jnp.zeros((slots, slots), F32)
    total = jnp.int32(0)
    for owner in range(owners):
        held = counts_ref[0, owner]
        first = (my_unit ^ owner) * capacity
        hit = (row_at >= first) & (row_at < first + held) & (slot_at - row_at == total - first)
        pick = jnp.where(hit, 1.0, pick)
        total = total + held
    return pick


def token_selector(assign_ref, units, capacity, my_unit):
    bits = bits_of(units)
    width, tokens = assign_ref.shape
    slices = units // min(LAYER_EXPERTS, units)
    dims = (tokens, units * capacity)
    token_at = lax.broadcasted_iota(jnp.int32, dims, 0)
    column_at = lax.broadcasted_iota(jnp.int32, dims, 1)
    selector = jnp.zeros(dims, F32)
    for token in range(tokens):
        for k in range(width):
            expert = assign_ref[k, token]
            rank = jnp.int32(0)
            for earlier in range(token):
                for other in range(width):
                    rank = rank + (assign_ref[other, earlier] == expert).astype(jnp.int32)
            for piece in range(slices):
                apart = (expert * slices + piece) ^ my_unit
                place = jnp.int32(0)
                for bit in range(bits):
                    place = place * 2 + (lax.shift_right_logical(apart, jnp.int32(bit)) & 1)
                hit = (token_at == token) & (column_at == place * capacity + rank)
                selector = jnp.where(hit, selector + 1.0, selector)
    return selector


def forward_kernel(units, *refs):
    x_hbm, dy_hbm, w_in_hbm, w_out_hbm, counts_hbm, assign_hbm = refs[:6]
    acts_ref, grad_ref, selector_ref, w_in_ref = refs[6:10]
    x_ref, dy_ref, w_out_ref, counts_ref, assign_ref, sems = refs[10:]
    hidden_units = w_out_ref.shape[0]
    used = []

    def begin(source, target):
        copy = pltpu.make_async_copy(source, target, sems.at[len(used)])
        copy.start()
        used.append(copy)
        return copy

    counts_copy = begin(counts_hbm, counts_ref)
    dy_copy = begin(dy_hbm, dy_ref)
    x_copy = begin(x_hbm, x_ref)
    out_cuts, cuts = step_cuts(hidden_units), step_cuts(2 * hidden_units)
    out_copies = [
        begin(w_out_hbm.at[pl.ds(at, size), :], w_out_ref.at[pl.ds(at, size), :])
        for at, size in out_cuts
    ]
    in_copies = [
        begin(w_in_hbm.at[pl.ds(at, size), :], w_in_ref.at[pl.ds(at, size), :])
        for at, size in cuts
    ]
    assign_copy = begin(assign_hbm, assign_ref)

    slots = x_ref.shape[0]
    capacity = slots // counts_ref.shape[1]
    my_unit = lax.axis_index("expert")
    counts_copy.wait()
    pick = pick_matrix(counts_ref, slots, my_unit)
    back = pick.T.astype(BF16)
    pick = pick.astype(BF16)
    dy_copy.wait()
    dy = jnp.dot(pick, dy_ref[...], preferred_element_type=F32).astype(BF16)
    x_copy.wait()
    x = jnp.dot(pick, x_ref[...], preferred_element_type=F32).astype(BF16)

    def product(rows, weights_ref, pieces, copies):
        found = []
        for (at, size), copy in zip(pieces, copies):
            copy.wait()
            found.append(
                lax.dot_general(
                    rows,
                    weights_ref[pl.ds(at, size), :],
                    CONTRACT_LAST,
                    preferred_element_type=F32,
                )
            )
        return jnp.concatenate(found, axis=1)

    grad_hidden = product(dy, w_out_ref, out_cuts, out_copies)
    pre = product(x, w_in_ref, cuts, in_copies)
    gate_pre, up_pre = pre[:, :hidden_units], pre[:, hidden_units:]
    sigmoid_gate = jax.nn.sigmoid(gate_pre)
    hidden = gate_pre * sigmoid_gate * up_pre
    grad_gate = grad_hidden * up_pre * sigmoid_gate * (1.0 + gate_pre * (1.0 - sigmoid_gate))
    grad_up = grad_hidden * gate_pre * sigmoid_gate
    acts = jnp.concatenate([grad_gate, grad_up, hidden], axis=1).astype(BF16)
    acts_ref[...] = jnp.dot(back, acts, preferred_element_type=F32).astype(BF16)
    grad_ref[...] = acts[:, : 2 * hidden_units]
    assign_copy.wait()
    selector_ref[...] = token_selector(assign_ref, units, capacity, my_unit)


def rows_kernel(parts, grad_ref, w_in_ref, keep_ref, send_ref, rows_ref):
    width = w_in_ref.shape[1]
    for at, size in cuts_of(width, 1024, 128):
        rows_ref[:, pl.ds(at, size)] = jnp.dot(
            grad_ref[...], w_in_ref[:, pl.ds(at, size)], preferred_element_type=F32
        )
    my_part = lax.axis_index("mp")
    bits = bits_of(parts)
    keep_ref[...] = rows_ref[:, lanes(column_start(my_part, bits, 0, width, False), width // 2)]
    send_ref[...] = rows_ref[
        :, lanes(column_start(my_part, bits, 0, width, True), width // 2)
    ].astype(BF16)


def sum_task(bits, step, width):
    def body(ins, outs):
        keep_ref, recv_ref = ins
        total = keep_ref[...].astype(F32) + recv_ref[...].astype(F32)
        if step + 1 < bits:
            me = lax.axis_index("mp")
            base = column_start(me, bits, step, width, False)
            size = width // 2 ** (step + 2)
            is_high = column_start(me, bits, step + 1, width, False) - base > 0
            low, high = total[:, :size], total[:, size:]
            outs[0][...] = jnp.where(is_high, high, low)
            outs[1][...] = jnp.where(is_high, low, high).astype(BF16)
        else:
            half = total.shape[0] // 2
            outs[0][...] = total[:half]
            outs[1][...] = total[half:].astype(BF16)

    return body


def deal_task(blocks, block):
    def body(ins, outs):
        keep, recv = ins[0][...].astype(F32), ins[1][...].astype(F32)
        joined = []
        for at in range(blocks):
            joined += [keep[at * block : (at + 1) * block], recv[at * block : (at + 1) * block]]
        outs[0][...] = jnp.concatenate(joined[:blocks], axis=0)
        outs[1][...] = jnp.concatenate(joined[blocks:], axis=0).astype(BF16)

    return body


def stack_task(ins, outs):
    at = 0
    for ref in ins:
        outs[0][pl.ds(at, ref.shape[0]), :] = ref[...]
        at += ref.shape[0]


def columns_task(bits, step, width):
    def body(ins, outs):
        me = lax.axis_index("dp")
        size = width // 2 ** (step + 1)
        start = column_start(me, bits, step, width, True)
        rows = ins[0].shape[0]
        outs[0][pl.ds(0, rows), :] = ins[0][...]
        at = rows
        for past, ref in enumerate(ins[1:]):
            base = column_start(me, bits, past, width, False)
            outs[0][pl.ds(at, ref.shape[0]), :] = ref[:, lanes(start - base, size)]
            at += ref.shape[0]

    return body


def run_whole(body, ins, outs, name, after=None):
    extra = [] if after is None else [after]

    def kernel(*refs):
        body(refs[: len(ins)], refs[len(ins) + len(extra) :])

    return pl.pallas_call(
        kernel,
        out_shape=outs,
        in_specs=[IN_VMEM] * (len(ins) + len(extra)),
        out_specs=[IN_VMEM] * len(outs),
        compiler_params=params(),
        name=name,
    )(*ins, *extra)


def weights_kernel(bits, width, *refs):
    count = 1 + bits
    sent, acts = refs[:count], refs[count : 2 * count]
    in_hbm, out_hbm, in_ref, out_ref, sems = refs[2 * count :]
    slots = acts[0].shape[0]
    me = lax.axis_index("dp")
    quarter = width // 2**bits
    x, dy = [], []
    for index, ref in enumerate(sent):
        if index == 0:
            block = ref[...]
        else:
            base = column_start(me, bits, index - 1, width, False)
            block = ref[:, lanes(me * quarter - base, quarter)]
        for at in range(0, block.shape[0], 2 * slots):
            x.append(block[at : at + slots])
            dy.append(block[at + slots : at + 2 * slots])
    x, dy = jnp.concatenate(x, axis=0), jnp.concatenate(dy, axis=0)
    columns = jnp.concatenate([ref[...] for ref in acts], axis=0).T
    copies = []

    def begin(source, target):
        copy = pltpu.make_async_copy(source, target, sems.at[len(copies)])
        copy.start()
        copies.append(copy)

    start = 0
    for values, target, staged in ((x, in_hbm, in_ref), (dy, out_hbm, out_ref)):
        for at, size in cuts_of(target.shape[0]):
            here = pl.ds(at, size)
            staged[here, :] = jnp.dot(
                columns[start + at : start + at + size], values, preferred_element_type=F32
            ).astype(BF16)
            begin(staged.at[here, :], target.at[here, :])
        start += target.shape[0]
    for copy in copies:
        copy.wait()


def tokens_kernel(selector_ref, keep_ref, recv_ref, out_ref):
    rows = jnp.concatenate([keep_ref[...].astype(F32), recv_ref[...].astype(F32)], axis=0)
    out_ref[...] = jnp.dot(
        selector_ref[...].astype(BF16), rows.astype(BF16), preferred_element_type=F32
    ).astype(BF16)


def in_hbm(array):
    return pltpu.with_memory_space_constraint(array, pltpu.HBM)


def swap(array, axis, bit):
    return lax.ppermute(array, axis, [(i, i ^ bit) for i in range(lax.axis_size(axis))])


def per_device(x_rows, dy_rows, w_in, w_out, counts, assign):
    slots, width = x_rows.shape
    hidden_units = w_out.shape[2]
    groups = lax.axis_size("dp")
    units = lax.axis_size("expert")
    parts = lax.axis_size("mp")
    owners = counts.shape[1]
    capacity = slots // owners
    quarter = width // groups
    share = width // parts
    dp_bits, unit_bits, part_bits = bits_of(groups), bits_of(units), bits_of(parts)

    split = pl.pallas_call(
        functools.partial(split_kernel, dp_bits),
        out_shape=[shape((2 * slots, width // 2 ** (i + 1))) for i in range(dp_bits)]
        + [shape((2 * slots, quarter))],
        in_specs=[IN_HBM, IN_HBM],
        out_specs=[ANY] * (dp_bits + 1),
        scratch_shapes=[pltpu.SemaphoreType.DMA((2 * dp_bits + 2,))],
        compiler_params=params(),
        cost_estimate=pl.CostEstimate(flops=0, bytes_accessed=2**19, transcendentals=0),
        name="split_rows",
    )(in_hbm(x_rows), in_hbm(dy_rows))
    sent = [split[dp_bits], swap(split[0], "dp", groups // 2)]

    w_flat = jnp.transpose(w_in[0], (1, 2, 0)).reshape(2 * hidden_units, width)
    w_down = jnp.transpose(w_out[0], (1, 0))
    acts, grad_pre, selector, w_kept = pl.pallas_call(
        functools.partial(forward_kernel, units),
        out_shape=[
            pltpu.VMEM((slots, 3 * hidden_units), BF16),
            pltpu.VMEM((slots, 2 * hidden_units), BF16),
            pltpu.VMEM((assign.shape[0], slots), F32),
            pltpu.VMEM(w_flat.shape, BF16),
        ],
        in_specs=[IN_HBM] * 6,
        out_specs=[IN_VMEM] * 4,
        scratch_shapes=[
            pltpu.VMEM(x_rows.shape, BF16),
            pltpu.VMEM(dy_rows.shape, BF16),
            pltpu.VMEM(w_down.shape, BF16),
            pltpu.SMEM(counts.shape, jnp.int32),
            pltpu.SMEM(assign.shape[::-1], jnp.int32),
            pltpu.SemaphoreType.DMA(
                (4 + len(step_cuts(hidden_units)) + len(step_cuts(2 * hidden_units)),)
            ),
        ],
        compiler_params=params(),
        cost_estimate=pl.CostEstimate(
            flops=2 * 256 * width * 3 * hidden_units,
            bytes_accessed=6 * hidden_units * width,
            transcendentals=0,
        ),
        name="forward",
    )(
        in_hbm(x_rows),
        in_hbm(dy_rows),
        in_hbm(w_flat),
        in_hbm(w_down),
        in_hbm(counts),
        in_hbm(assign.T),
    )
    keep, send = pl.pallas_call(
        functools.partial(rows_kernel, parts),
        out_shape=[shape((slots, width // 2), F32), shape((slots, width // 2))],
        in_specs=[IN_VMEM] * 2,
        out_specs=[IN_VMEM] * 2,
        scratch_shapes=[pltpu.VMEM((slots, width), F32)],
        compiler_params=params(),
        cost_estimate=pl.CostEstimate(
            flops=2 * slots * width * 2 * hidden_units, bytes_accessed=0, transcendentals=0
        ),
        name="row_grads",
    )(grad_pre, w_kept)

    acts_all = [acts]
    swaps = [("mp", parts >> (i + 1)) for i in range(part_bits)]
    swaps += [("expert", units >> (i + 1)) for i in range(unit_bits)]
    rows_held = slots
    for step in range(max(len(swaps), dp_bits)):
        if 0 < step < dp_bits:
            (columns,) = run_whole(
                columns_task(dp_bits, step, width),
                [split[step]] + sent[1:],
                [shape((2 * slots << step, width >> (step + 1)))],
                "columns%d" % step,
                after=acts_all[-1],
            )
            sent.append(swap(columns, "dp", groups >> (step + 1)))
        if 0 < step < len(swaps):
            if step <= part_bits:
                body = sum_task(part_bits, step - 1, width)
                out = (slots, width >> (step + 1)) if step < part_bits else (slots // 2, share)
            else:
                past = step - part_bits
                body = deal_task(owners >> past, capacity << (past - 1))
                out = (slots // 2, share)
            keep, send = run_whole(body, [keep, recv], [shape(out, F32), shape(out)], "rows%d" % step)
        if step < len(swaps):
            recv = swap(send, *swaps[step])
        if step < dp_bits:
            held = acts
            if step > 0:
                (held,) = run_whole(
                    stack_task,
                    acts_all,
                    [shape((slots << step, 3 * hidden_units))],
                    "acts%d" % step,
                )
            acts_all.append(swap(held, "dp", groups >> (step + 1)))

    grad_in, grad_out = pl.pallas_call(
        functools.partial(weights_kernel, dp_bits, width),
        out_shape=[
            shape((2 * hidden_units, quarter)),
            shape((hidden_units, quarter)),
        ],
        in_specs=[IN_VMEM] * (2 + 2 * dp_bits),
        out_specs=[ANY] * 2,
        scratch_shapes=[
            pltpu.VMEM((2 * hidden_units, quarter), BF16),
            pltpu.VMEM((hidden_units, quarter), BF16),
            pltpu.SemaphoreType.DMA(
                (len(cuts_of(2 * hidden_units)) + len(cuts_of(hidden_units)),)
            ),
        ],
        compiler_params=params(),
        cost_estimate=pl.CostEstimate(
            flops=2 * 256 * quarter * 3 * hidden_units,
            bytes_accessed=6 * hidden_units * quarter,
            transcendentals=0,
        ),
        name="weight_grads",
    )(*sent, *acts_all)

    grad_tokens = pl.pallas_call(
        tokens_kernel,
        out_shape=shape((assign.shape[0], share)),
        in_specs=[IN_VMEM] * 3,
        out_specs=IN_VMEM,
        compiler_params=params(),
        name="token_grads",
    )(selector, keep, recv)

    grad_w_in = grad_in.reshape(2, hidden_units, quarter).transpose(2, 0, 1)[None]
    grad_w_out = grad_out.transpose(1, 0)[None]
    return (grad_w_in, grad_w_out, grad_tokens)


def solution(mesh):
    return jax.shard_map(
        per_device,
        mesh=mesh,
        in_specs=(
            P(("dp", "expert"), None),
            P(("dp", "expert"), None),
            P("expert", None, None, "mp"),
            P("expert", None, "mp"),
            P(("dp", "expert"), None),
            P(("dp", "expert"), None),
        ),
        out_specs=(
            P("expert", "dp", None, "mp"),
            P("expert", "dp", "mp"),
            P(("dp", "expert"), "mp"),
        ),
        check_vma=False,
    )
```
